256 devices in a mesh: dp: 16 (over z, y_hi), et: 16 (over y_lo, x, core).
Axes of the slice: x: 4, y: 4 (y_hi: 2, y_lo: 2; y = y_hi * 2 + y_lo), z: 8, core: 2. Of those that a mesh axis runs over, the one named last changes fastest.
Arguments:
- tokens: bfloat16 [16, 2048, 3072], P('dp', 'et'), may hold values from -6 to 6
- cotangent: bfloat16 [16, 2048, 3072], P('dp', 'et'), may hold values from -6 to 6
- route_ids: int32 [16, 2048, 2], P('dp', 'et'), may hold values from 0 to 7, as said below
- route_weight: bfloat16 [16, 2048, 2], P('dp', 'et'), may hold values from 0.25 to 1
- segment_ids: int32 [16, 2048], P('dp', 'et'), may hold values from 0 to 7, never falling along the last dimension, each value on 1 to 512 neighbouring positions
- gate_weight: bfloat16 [3072, 8192], P(None, 'et'), may hold values from -0.109375 to 0.109375
- up_weight: bfloat16 [3072, 8192], P(None, 'et'), may hold values from -0.109375 to 0.109375
- down_weight: bfloat16 [3072, 8192], P(None, 'et'), may hold values from -0.0625 to 0.0625
Outputs:
- grad_tokens: bfloat16 [16, 2048, 3072], P('dp', 'et')
- grad_route: float32 [16, 2048], P('dp', 'et')
- grad_gate: float32 [3072, 8192], P('dp', 'et')
- grad_up: float32 [3072, 8192], P('dp', 'et')
- grad_down: float32 [3072, 8192], P('dp', 'et')
The draws below stay inside these ranges and needn't reach their ends.
Inputs may be any that keep to these rules, and one draw needn't show every extreme that they name: `route_ids`: each token names two different experts. Among the tokens of one device at most 32 and at least one name expert 0; in every draw the tokens of some device name it exactly 32 times.
All inputs are finite; a program needn't handle non-finite values.
Results may differ from the reference program's by a relative error of at most 0.0058.
Values may be sent and summed in bfloat16 or wider, within the bound.
A program may use at most 192 MiB of HBM per device.

```python
import math
import jax
import jax.numpy as jnp
import numpy as np
from jax import lax

D = 3072
EXPERTS = 8
TOP = 2
SEGS = 8
TOK_DEV = 128
CAP = 32
GROUP_TOK = 2048
FF = 8192
N_DP = 16
N_ET = 16


def draw_route_ids(key, part):
    key = jax.random.fold_in(key, 11)
    blocks = N_DP * N_ET
    keys = jax.random.split(key, 6)
    counts = jax.random.randint(keys[0], (blocks,), 1, CAP + 1)
    fullest = jax.random.randint(keys[1], (), 0, blocks)
    counts = jnp.where(jnp.arange(blocks, dtype=jnp.int32) == fullest, CAP, counts)
    order = jax.vmap(lambda single: jax.random.permutation(single, TOK_DEV))(jax.random.split(keys[2], blocks))
    sorted_flag = (jnp.arange(TOK_DEV, dtype=jnp.int32)[None, :] < counts[:, None]).astype(jnp.int32)
    routed = jnp.zeros((blocks, TOK_DEV), jnp.int32).at[jnp.arange(blocks, dtype=jnp.int32)[:, None], order].set(sorted_flag)
    other = jax.random.randint(keys[3], (blocks, TOK_DEV), 1, EXPERTS)
    second = 1 + (other - 1 + jax.random.randint(keys[4], (blocks, TOK_DEV), 1, EXPERTS - 1)) % (EXPERTS - 1)
    first_col = jnp.where(routed == 1, 0, other)
    second_col = jnp.where(routed == 1, other, second)
    swapped = jax.random.randint(keys[5], (blocks, TOK_DEV), 0, 2)
    left = jnp.where(swapped == 1, second_col, first_col)
    right = jnp.where(swapped == 1, first_col, second_col)
    return jnp.stack([left, right], axis=-1).reshape(N_DP, GROUP_TOK, TOP).astype(jnp.int32)


def spiked(array, stream_key, source, target, parts, factor):
    def block_of(dim):
        return (jnp.arange(array.shape[dim]) // (array.shape[dim] // parts)).reshape((-1,) + (1,) * (array.ndim - 1 - dim))

    one_side = jax.random.permutation(stream_key, parts)[block_of(target)]
    other_side = (block_of(target) + parts // 2) % parts
    return jnp.where((block_of(source) == one_side) | (block_of(source) == other_side), factor * array, array)


def block_levels(key, shape, cuts, smallest, top_value):
    def one(position, blocks):
        draws = jax.random.uniform(jax.random.fold_in(jax.random.fold_in(key, 6), position), (blocks,), jnp.float32, smallest / len(cuts), top_value / len(cuts))
        return jnp.repeat(jnp.exp(draws), shape[position] // blocks).reshape((-1,) + (1,) * (len(shape) - position - 1))

    gain = one(*cuts[0])
    for cut in cuts[1:]:
        gain = gain * one(*cut)
    return gain


def profile(amount, total, limit, lean):
    weights = [(1 << 20) // math.isqrt(standing ** lean) + 1 for standing in range(2, amount + 1)]
    rest, holding = total - limit - (amount - 1), [1] * (amount - 1)
    while rest > 0:
        free = [i for i in range(amount - 1) if holding[i] < limit]
        mass, budget = sum([weights[i] for i in free]), rest
        for i in free:
            more = min(limit - holding[i], max(1, budget * weights[i] // mass), rest)
            holding[i] = holding[i] + more
            rest = rest - more
    return np.array([limit] + holding)


def ragged(key, count, total, most, skew):
    if count == 2:
        one = jax.random.randint(key, (), max(1, total - most), min(most, total - 1) + 1)
        return jnp.stack([one, total - one])
    sizes = jnp.asarray(profile(count, total, most, skew), jnp.int32)
    couples = (count - 1) // 2
    source_of, taker = sizes[1:1 + 2 * couples:2], sizes[2:2 + 2 * couples:2]
    room = jnp.minimum(source_of - 1, most - taker)
    passed = jax.random.randint(jax.random.fold_in(key, 1), (couples,), 0, 1 << 20) % (room + 1)
    sizes = sizes.at[1:1 + 2 * couples:2].set(source_of - passed).at[2:2 + 2 * couples:2].set(taker + passed)
    return sizes[jax.random.permutation(jax.random.fold_in(key, 2), count)]


def scatter_about(rng, dims, width, bound, cuts=(), kind=jnp.bfloat16):
    entries = width * jax.random.normal(rng, dims, jnp.float32)
    if cuts:
        entries = entries * block_levels(rng, dims, cuts, -0.22, 0.18)
    return jnp.clip(entries, -bound, bound).astype(kind)


def gaussian_with(own_key, dims, width, limit, cuts, heavy, kind=jnp.bfloat16):
    values = width * jax.random.normal(own_key, dims, jnp.float32)
    if cuts:
        values = values * block_levels(own_key, dims, cuts, -0.22, 0.18)
    return jnp.clip(spiked(values, jax.random.fold_in(own_key, 3), *heavy), -limit, limit).astype(kind)


def setup_inputs(seed: int = 0) -> dict:
    key_list = jax.random.split(jax.random.key(seed), 9)
    tokens = gaussian_with(key_list[0], (N_DP, GROUP_TOK, D), 1.0, 6.0, ((0, 16), (1, 16)), (0, 2, 16, 2.0))
    cotangent = gaussian_with(key_list[1], (N_DP, GROUP_TOK, D), 1.0, 6.0, ((0, 16), (1, 16)), (0, 2, 16, 2.0))
    route_ids = draw_route_ids(jax.random.fold_in(key_list[8], 71), 0)
    route_weight = jnp.clip(0.25 + 0.75 * jax.random.uniform(key_list[3], (N_DP, GROUP_TOK, TOP), jnp.float32) ** block_levels(key_list[3], (N_DP, GROUP_TOK, TOP), ((0, 16), (1, 16)), -0.2, 0.2), 0.25, 1.0).astype(jnp.bfloat16)
    segment_ids = jax.vmap(lambda own: jnp.searchsorted(jnp.cumsum(ragged(own, SEGS, GROUP_TOK, GROUP_TOK // 4, 2)), jnp.arange(GROUP_TOK), side="right"))(jax.random.split(key_list[4], N_DP)).reshape((N_DP, GROUP_TOK)).astype(jnp.int32)
    gate_weight = scatter_about(key_list[5], (D, FF), D ** -0.5, 0.109375, ((1, 16),))
    up_weight = scatter_about(key_list[6], (D, FF), D ** -0.5, 0.109375, ((1, 16),))
    down_weight = scatter_about(key_list[7], (D, FF), FF ** -0.5, 0.0625, ((1, 16),))
    return {"tokens": tokens, "cotangent": cotangent, "route_ids": route_ids, "route_weight": route_weight, "segment_ids": segment_ids, "gate_weight": gate_weight, "up_weight": up_weight, "down_weight": down_weight}


def silu_pieces(preact):
    sigmoid_val = jax.nn.sigmoid(preact)
    return preact * sigmoid_val, sigmoid_val * (1.0 + preact * (1.0 - sigmoid_val))


def contract_rows(left, right):
    return lax.dot_general(left, right, (((0,), (0,)), ((), ())), preferred_element_type=jnp.float32)


def contract_cols(left, right):
    return lax.dot_general(left, right, (((1,), (1,)), ((), ())), preferred_element_type=jnp.float32)


def expert_backward(rows_in, rows_cot, slot_prob, gate_weight, up_weight, down_weight):
    gate_pre = jnp.dot(rows_in, gate_weight, preferred_element_type=jnp.float32)
    up_pre = jnp.dot(rows_in, up_weight, preferred_element_type=jnp.float32)
    active, slope_val = silu_pieces(gate_pre)
    hidden = active * up_pre
    backed = jnp.dot(rows_cot, down_weight, preferred_element_type=jnp.float32)
    route_part = jnp.sum(hidden * backed, axis=1)
    scaled_back = slot_prob[:, None] * backed
    grad_gate_rows = (scaled_back * up_pre * slope_val).astype(jnp.bfloat16)
    grad_up_rows = (scaled_back * active).astype(jnp.bfloat16)
    held_rows = (slot_prob[:, None] * hidden).astype(jnp.bfloat16)
    input_grad = contract_cols(grad_gate_rows, gate_weight) + contract_cols(grad_up_rows, up_weight)
    return route_part, grad_gate_rows, grad_up_rows, held_rows, input_grad


def pack_index(routed, total_slots):
    slot_pos = jnp.cumsum(routed.astype(jnp.int32)) - 1
    target = jnp.where(routed, slot_pos, total_slots).astype(jnp.int32)
    row_index = jnp.zeros((total_slots,), jnp.int32).at[target].set(jnp.arange(routed.shape[0], dtype=jnp.int32), mode="drop")
    live_slot = jnp.arange(total_slots, dtype=jnp.int32) < jnp.sum(routed.astype(jnp.int32))
    return row_index, live_slot


def rounded_partial(value):
    return lax.optimization_barrier(value.astype(jnp.bfloat16)).astype(jnp.float32)


def reference(tokens, cotangent, route_ids, route_weight, segment_ids, gate_weight, up_weight, down_weight):
    total_slots = N_ET * CAP
    labels = jnp.arange(SEGS, dtype=jnp.int32)

    def group_step(running, pieces):
        group_in, group_cot, group_ids, group_weight, group_seg = pieces
        member = (group_seg[:, None] == labels[None, :]).astype(jnp.float32)
        counts = jnp.sum(member, axis=0)
        weight = 1.0 / jnp.sum(member * counts[None, :], axis=1)
        scaled = (group_cot.astype(jnp.float32) * weight[:, None]).astype(jnp.bfloat16)
        chosen = group_ids == 0
        route_prob = jnp.sum(jnp.where(chosen, group_weight.astype(jnp.float32), 0.0), axis=1)
        routed = jnp.any(chosen, axis=1)
        row_index, live_slot = pack_index(routed, total_slots)
        rows_in = group_in[row_index]
        rows_cot = scaled[row_index]
        slot_prob = jnp.where(live_slot, route_prob[row_index], 0.0)
        route_part, grad_gate_rows, grad_up_rows, held_rows, input_grad = expert_backward(
            rows_in, rows_cot, slot_prob, gate_weight, up_weight, down_weight)
        grad_rows = jnp.zeros((GROUP_TOK, D), jnp.float32).at[row_index].add(jnp.where(live_slot[:, None], input_grad, 0.0))
        route_rows = jnp.zeros((GROUP_TOK,), jnp.float32).at[row_index].add(jnp.where(live_slot, route_part, 0.0))
        sum_gate, sum_up, sum_down = running
        sum_gate = sum_gate + rounded_partial(contract_rows(rows_in, grad_gate_rows))
        sum_up = sum_up + rounded_partial(contract_rows(rows_in, grad_up_rows))
        sum_down = sum_down + rounded_partial(contract_rows(rows_cot, held_rows))
        return (sum_gate, sum_up, sum_down), (grad_rows.astype(jnp.bfloat16), route_rows)

    empty = jnp.zeros((D, FF), jnp.float32)
    sums, outputs = lax.scan(group_step, (empty, empty, empty), (tokens, cotangent, route_ids, route_weight, segment_ids))
    return outputs[0], outputs[1], sums[0], sums[1], sums[2]
```

```python
import jax
import jax.numpy as jnp
from jax import lax
from jax.experimental import pallas as pl
from jax.experimental.pallas import tpu as pltpu
from jax.sharding import PartitionSpec as P

MESH = pl.DeviceIdType.MESH
F32 = jnp.float32
BF16 = jnp.bfloat16
NZ = 8
QW = 768
ZW = 384
FH = 256
SL = 32


def nn(a, b):
    return jnp.dot(a, b, preferred_element_type=F32)


def nt(a, b):
    return lax.dot_general(a, b, (((1,), (1,)), ((), ())), preferred_element_type=F32)


def wrap(v, n):
    return lax.rem(v + 2 * n, n)


def kernel(
    tok_ref, cot_ref, ids_ref, rw_ref, seg_ref, wg_hbm, wu_hbm, wd_hbm,
    gt_ref, gr_ref, gg_ref, gu_ref, gd_ref,
    tb, cb, meta, cnt, wgu, wd, pre, dgu, dT, zs, zr, sgs, sgr, p1s, p1r, p2s, p2r, g2,
    q1s, q1r, q2s, q2r, fin, fing, rps, rpr, fsum, fxs, fxr,
    w_sem, ag_s, ag_r, sib_s, sib_r, m_s, m_r, z_s, z_r, g_s, g_r, rt_s, rt_r, fx_s, fx_r,
):
    dp, et = lax.axis_index("dp"), lax.axis_index("et")
    z, yh = lax.div(dp, 2), lax.rem(dp, 2)
    yl, x, c = lax.div(et, 8), lax.rem(lax.div(et, 2), 4), lax.rem(et, 2)
    y = yh * 2 + yl
    p, r = y + c * (x - y), x + c * (y - x)

    def dev(xx, yy, zz, cc):
        return (zz * 2 + lax.div(yy, 2), lax.rem(yy, 2) * 8 + xx * 2 + cc)

    def at(dp_, dr_):
        pp, rr = wrap(p + dp_, 4), wrap(r + dr_, 4)
        return dev(rr + c * (pp - rr), pp + c * (rr - pp), z, c)

    def pos(dp_, dr_):
        return wrap(p + dp_, 4) * 4 + wrap(r + dr_, 4)

    sib = dev(x, y, z, 1 - c)
    zplus, zminus = dev(x, y, wrap(z + 1, NZ), c), dev(x, y, wrap(z - 1, NZ), c)

    def flip(v, bit):
        return v + bit - 2 * bit * lax.rem(lax.div(v, bit), 2)

    hyper = [sib, dev(flip(x, 1), y, z, c), dev(flip(x, 2), y, z, c),
             dev(x, flip(y, 1), z, c), dev(x, flip(y, 2), z, c)]
    partner = hyper[4]

    half = pl.ds(pl.multiple_of(yh * FH, FH), FH)
    wcopies = [
        pltpu.make_async_copy(wg_hbm.at[:, half], wgu.at[:, pl.ds(0, FH)], w_sem.at[0]),
        pltpu.make_async_copy(wu_hbm.at[:, half], wgu.at[:, pl.ds(FH, FH)], w_sem.at[1]),
        pltpu.make_async_copy(wd_hbm.at[:, half], wd, w_sem.at[2]),
    ]
    for cp in wcopies:
        cp.start()

    barrier = pltpu.get_barrier_semaphore()
    for nb in (sib, at(1, 0), at(-1, 0), at(0, 1), at(0, -1), at(2, 0), at(0, 2), zplus, zminus):
        pl.semaphore_signal(barrier, inc=1, device_id=nb, device_id_type=MESH)

    sent = []

    def copy(src, dst, ss, rs, to):
        return pltpu.make_async_remote_copy(
            src_ref=src, dst_ref=dst, send_sem=ss, recv_sem=rs, device_id=to, device_id_type=MESH)

    def send(src, dst, ss, rs, to):
        cp = copy(src, dst, ss, rs, to)
        cp.start()
        sent.append(cp)

    def arrived(ref, ss, rs):
        copy(ref, ref, ss, rs, sib).wait_recv()

    n = 128
    row_i = lax.broadcasted_iota(jnp.int32, (n, n), 0)
    col_i = lax.broadcasted_iota(jnp.int32, (n, n), 1)
    chosen = ids_ref[...] == 0
    routed = jnp.max(chosen.astype(F32), axis=1, keepdims=True)
    prob = jnp.sum(jnp.where(chosen, rw_ref[...].astype(F32), 0.0), axis=1, keepdims=True)
    routed_c = jnp.broadcast_to(routed, (n, n))
    routed_r = routed_c.T
    before = (row_i < col_i).astype(F32).astype(BF16)
    after = (col_i < row_i).astype(F32).astype(BF16)
    slot_r = nn(routed_r.astype(BF16), before)
    slot_c = nn(after, routed_c.astype(BF16))
    pick = jnp.where((slot_r == row_i.astype(F32)) & (routed_r > 0.5), 1.0, 0.0)[:SL].astype(BF16)
    place = jnp.where((slot_c == col_i.astype(F32)) & (routed_c > 0.5), 1.0, 0.0)[:, :SL].astype(BF16)

    mine = pl.ds(pl.multiple_of(c * SL, SL), SL)
    here = p * 4 + r
    there = r * 4 + p

    def pack(src, buf):
        for h in range(2):
            for q in range(2):
                cols = slice((h * 2 + q) * QW, (h * 2 + q + 1) * QW)
                buf[h, here, q, mine, :] = nn(pick, src[:, cols]).astype(BF16)

    def swap(t, buf):
        for k, h in ((0, 1 - c), (1, c)):
            send(buf.at[h, here, :, mine, :], buf.at[h, there, :, mine, :],
                 sib_s.at[t, 16 + k], sib_r.at[t, 16 + k], sib)

    other = pl.ds(pl.multiple_of((1 - c) * SL, SL), SL)

    def swapped(t, buf, k):
        h = c if k == 0 else 1 - c
        arrived(buf.at[h, here, :, other, :], sib_s.at[t, 16 + k], sib_r.at[t, 16 + k])

    me_idx = (y * 4 + x) * 2 + c
    seg = jnp.broadcast_to(seg_ref[...], (n, n))
    member = jnp.where(seg == row_i, 1.0, 0.0).astype(BF16)
    prob_m = jnp.where(col_i == 16, jnp.broadcast_to(prob, (n, n)), 0.0).astype(BF16)
    meta[me_idx, pl.ds(0, SL), :] = (nt(pick, member) + nn(pick, prob_m)).astype(BF16)
    meta[me_idx, pl.ds(SL, 16), :] = nt(jnp.ones((16, n), BF16), member).astype(BF16)

    pack(tok_ref, tb)
    pl.semaphore_wait(barrier, 9)
    swap(0, tb)

    def meta_send(k):
        size = 1 << k
        base = lax.div(me_idx, size) * size
        ref = meta.at[pl.ds(base, size)]
        send(ref, ref, m_s.at[k], m_r.at[k], hyper[k])

    def meta_got(k):
        size = 1 << k
        base = flip(lax.div(me_idx, size), 1) * size
        arrived(meta.at[pl.ds(base, size)], m_s.at[k], m_r.at[k])

    meta_send(0)
    pack(cot_ref, cb)

    line = (0, -1, 1, 2)

    def ag(t, buf):
        def one(dst_p, dst_r, q, k, to):
            ref = buf.at[c, pos(dst_p, dst_r)] if q is None else buf.at[c, pos(dst_p, dst_r), q]
            send(ref, ref, ag_s.at[t, k], ag_r.at[t, k], to)

        def got(dst_p, dst_r, q, k):
            ref = buf.at[c, pos(dst_p, dst_r)] if q is None else buf.at[c, pos(dst_p, dst_r), q]
            arrived(ref, ag_s.at[t, k], ag_r.at[t, k])

        def to_sib(a, b):
            k = (a % 4) * 4 + b % 4
            send(buf.at[c, pos(a, b)], buf.at[c, wrap(r + b, 4) * 4 + wrap(p + a, 4)],
                 sib_s.at[t, k], sib_r.at[t, k], sib)

        def out_p(j):
            one(0, line[j], None, 4 + 4 * j, at(1, 0))
            one(0, line[j], None, 5 + 4 * j, at(-1, 0))

        def begin():
            one(0, 0, None, 0, at(0, 1))
            one(0, 0, None, 1, at(0, -1))
            out_p(0)

        def first():
            got(0, -1, None, 0)
            one(0, -1, 0, 2, at(0, 1))
            out_p(1)
            to_sib(0, -1)
            got(0, 1, None, 1)
            one(0, 1, 1, 3, at(0, -1))
            out_p(2)
            to_sib(0, 1)

        def second():
            got(0, 2, 0, 2)
            got(0, 2, 1, 3)
            out_p(3)
            to_sib(0, 2)

        def near(j):
            got(-1, line[j], None, 4 + 4 * j)
            one(-1, line[j], 0, 6 + 4 * j, at(1, 0))
            to_sib(-1, line[j])
            got(1, line[j], None, 5 + 4 * j)
            one(1, line[j], 1, 7 + 4 * j, at(-1, 0))
            to_sib(1, line[j])

        def far(j):
            got(2, line[j], 0, 6 + 4 * j)
            got(2, line[j], 1, 7 + 4 * j)
            to_sib(2, line[j])

        def from_sib():
            for a in range(4):
                for b in range(4):
                    if a or b:
                        k = a * 4 + b
                        arrived(buf.at[1 - c, pos(b, a)], sib_s.at[t, k], sib_r.at[t, k])
            swapped(t, buf, 1)

        return begin, first, second, near, far, from_sib

    T, C = ag(0, tb), ag(1, cb)
    swapped(0, tb, 0)
    T[0]()
    swap(1, cb)
    meta_got(0)
    meta_send(1)
    T[1]()
    meta_got(1)
    meta_send(2)
    T[2]()
    swapped(1, cb, 0)
    meta_got(2)
    meta_send(3)
    T[3](0)
    C[0]()
    T[3](1)
    meta_got(3)
    meta_send(4)
    T[4](0)
    T[3](2)
    T[4](1)
    T[3](3)
    T[4](2)
    T[4](3)
    C[1]()
    T[5]()
    C[2]()
    meta_got(4)

    for g in range(2):
        cnt[g] = jnp.sum(meta[pl.ds(16 * g, 16), pl.ds(SL, 16), :].astype(F32), axis=0)[:8]

    for cp in wcopies:
        cp.wait()

    def fwd(i):
        rows = pl.ds(pl.multiple_of(i * 256, 256), 256)
        acc = None
        for h in range(2):
            for q in range(2):
                xs = tb[h, pl.ds(i * 4, 4), q].reshape(256, QW)
                part = nn(xs, wgu[(h * 2 + q) * QW:(h * 2 + q + 1) * QW, :])
                acc = part if acc is None else acc + part
        pre[rows, :] = acc

    C[3](0)
    fwd(0)
    C[3](1)
    C[4](0)
    fwd(1)
    C[3](2)
    C[4](1)
    fwd(2)
    C[3](3)
    C[4](2)
    fwd(3)
    C[4](3)
    C[5]()

    lane = lax.broadcasted_iota(jnp.int32, (n, n), 1)

    @pl.loop(0, 8)
    def _(j):
        rows = pl.ds(pl.multiple_of(j * n, n), n)
        back = None
        for h in range(2):
            for q in range(2):
                xs = cb[h, pl.ds(j * 2, 2), q].reshape(n, QW)
                part = nn(xs, wd[(h * 2 + q) * QW:(h * 2 + q + 1) * QW, :])
                back = part if back is None else back + part
        chips, metas, counts = [], [], []
        for k in range(2):
            i = j * 2 + k
            chip = i + c * (lax.rem(i, 4) * 4 + lax.div(i, 4) - i)
            m = meta[pl.ds(chip * 2, 2), pl.ds(0, SL), :].astype(F32).reshape(2 * SL, n)
            chips.append(chip)
            metas.append(m)
            counts.append(jnp.where(lane[:64] < 8, m * cnt[lax.div(chip, 8)][0:1], 0.0))
        m = jnp.concatenate(metas, axis=0)
        count = jnp.sum(jnp.concatenate(counts, axis=0), axis=1, keepdims=True)
        weight = jnp.where(count > 0.0, 1.0 / jnp.maximum(count, 1.0), 0.0)
        pr = jnp.sum(jnp.where(lane == 16, m, 0.0), axis=1, keepdims=True)
        gate, up = pre[rows, 0:FH], pre[rows, FH:2 * FH]
        back = back * weight
        sg = 1.0 / (1.0 + jnp.exp(-gate))
        act = gate * sg
        slope = sg * (1.0 + gate * (1.0 - sg))
        hid = act * up
        rp = jnp.sum(hid * back, axis=1, keepdims=True)
        sb = back * pr
        dg = sb * up * slope
        du = sb * act
        he = hid * (pr * weight)
        dgu[lax.div(j, 2), lax.rem(j, 2), :, 0:FH] = dg.astype(BF16)
        dgu[lax.div(j, 2), lax.rem(j, 2), :, FH:2 * FH] = du.astype(BF16)
        dT[0:FH, rows] = dg.T.astype(BF16)
        dT[FH:2 * FH, rows] = du.T.astype(BF16)
        dT[2 * FH:3 * FH, rows] = he.T.astype(BF16)
        rp_row = jnp.broadcast_to(rp, (n, n)).T[0:1]
        rps[0, pl.ds(chips[0], 1), :] = jnp.where(lane[0:1] < 64, rp_row, 0.0)
        rps[0, pl.ds(chips[1], 1), :] = jnp.where(lane[0:1] < 64, pltpu.roll(rp_row, 64, 1), 0.0)

    def part(u, d):
        buf = cb if u == 2 else tb
        cols = pl.ds(pl.multiple_of(lax.rem(d, 2) * ZW, 128), ZW)
        xs = buf[lax.div(d, 4), :, lax.rem(lax.div(d, 2), 2), :, cols].reshape(1024, ZW)
        return nn(dT[u * FH:(u + 1) * FH, :], xs)

    units = (2, 0, 1)
    HF = FH // 2
    STEPS = NZ // 2

    def z_unit(s, u):
        if s == 1:
            val = part(u, wrap(z + STEPS, NZ)).astype(BF16)
            for dr, to in ((0, zplus), (1, zminus)):
                zs[dr, 0, u, dr * HF:(dr + 1) * HF, :] = val[dr * HF:(dr + 1) * HF]
                ref = (dr, 0, u, pl.ds(dr * HF, HF))
                send(zs.at[ref], zr.at[ref], z_s.at[dr, 0, u], z_r.at[dr, 0, u], to)
            return
        for dr, to, off in ((0, zplus, STEPS + 1 - s), (1, zminus, s - STEPS - 1)):
            val = part(u, wrap(z + off, NZ))
            if s == 2:
                ref = zr.at[dr, 0, u, pl.ds(dr * HF, HF)]
                arrived(ref, z_s.at[dr, 0, u], z_r.at[dr, 0, u])
                lo, hi = dr * HF, (dr + 1) * HF
                o_lo, o_hi = HF - lo, FH - lo
                zs[dr, 1, u, lo:hi, :] = (val[lo:hi] + ref[...].astype(F32)).astype(BF16)
                zs[dr, 1, u, o_lo:o_hi, :] = val[o_lo:o_hi].astype(BF16)
            else:
                ref = zr.at[dr, s - 2, u]
                arrived(ref, z_s.at[dr, s - 2, u], z_r.at[dr, s - 2, u])
                zs[dr, s - 1, u] = (val + ref[...].astype(F32)).astype(BF16)
            send(zs.at[dr, s - 1, u], zr.at[dr, s - 1, u], z_s.at[dr, s - 1, u], z_r.at[dr, s - 1, u], to)

    def z_step(s):
        for u in units:
            z_unit(s, u)

    outs = (gg_ref, gu_ref, gd_ref)
    mycols = pl.ds(pl.multiple_of(yh * FH, FH), FH)
    yourcols = pl.ds(pl.multiple_of((1 - yh) * FH, FH), FH)

    def z_last(u):
        val = part(u, z)
        for dr in range(2):
            ref = zr.at[dr, STEPS - 1, u]
            arrived(ref, z_s.at[dr, STEPS - 1, u], z_r.at[dr, STEPS - 1, u])
            val = val + ref[...].astype(F32)
        fsum[u] = val.T
        fxs[u] = fsum[u, pl.ds(pl.multiple_of((1 - yh) * 192, 192), 192), :].astype(BF16)
        send(fxs.at[u], fxr.at[u], fx_s.at[u], fx_r.at[u], partner)
        outs[u][:, mycols] = fsum[u, pl.ds(pl.multiple_of(yh * 192, 192), 192), :]

    def z_out(u):
        arrived(fxr.at[u], fx_s.at[u], fx_r.at[u])
        outs[u][:, yourcols] = fxr[u].astype(F32)

    def wrows(h, q):
        return wgu[pl.ds(pl.multiple_of((h * 2 + q) * QW, QW), QW), :]

    def g_sib(k):
        rr = wrap(r + (2, 1, -1, 0)[k], 4)
        j0, odd = lax.div(rr, 2), lax.rem(rr, 2)
        xs = dgu[:, j0, pl.ds(pl.multiple_of(odd * 64, 64), 64), :].reshape(256, 2 * FH)
        for q in range(2):
            sgs[rr, :, q] = nt(xs, wrows(1 - c, q)).astype(BF16).reshape(4, 64, QW)
        send(sgs.at[rr], sgr.at[rr], g_s.at[k], g_r.at[k], sib)

    def g_line(off, k):
        pp = wrap(p + off, 4)
        arrived(sgr.at[pp], g_s.at[k], g_r.at[k])
        xs = dgu[pp].reshape(256, 2 * FH)
        return [nt(xs, wrows(c, q)).reshape(4, 64, QW) + sgr[pp, :, q].astype(F32) for q in range(2)]

    def g1():
        val = g_line(2, 0)
        for q in range(2):
            p1s[q] = val[q].astype(BF16)
            send(p1s.at[q], p1r.at[q], g_s.at[4 + q], g_r.at[4 + q], at(1 - 2 * q, 0))

    def g_2(q):
        val = g_line(1 - 2 * q, 1 + q)
        arrived(p1r.at[q], g_s.at[4 + q], g_r.at[4 + q])
        p2s[q, :, q] = (val[q] + p1r[q].astype(F32)).astype(BF16)
        p2s[q, :, 1 - q] = val[1 - q].astype(BF16)
        send(p2s.at[q], p2r.at[q], g_s.at[6 + q], g_r.at[6 + q], at(1 - 2 * q, 0))

    def g3():
        val = g_line(0, 3)
        for q in range(2):
            arrived(p2r.at[q], g_s.at[6 + q], g_r.at[6 + q])
        for q in range(2):
            g2[:, q] = val[q] + p2r[0, :, q].astype(F32) + p2r[1, :, q].astype(F32)
        opp = wrap(r + 2, 4)
        for q in range(2):
            q1s[q] = g2[opp, q].astype(BF16)
            send(q1s.at[q], q1r.at[q], g_s.at[8 + q], g_r.at[8 + q], at(0, 1 - 2 * q))

    def g4():
        for q in range(2):
            rr = wrap(r + 1 - 2 * q, 4)
            arrived(q1r.at[q], g_s.at[8 + q], g_r.at[8 + q])
            q2s[q, q] = (g2[rr, q] + q1r[q].astype(F32)).astype(BF16)
            q2s[q, 1 - q] = g2[rr, 1 - q].astype(BF16)
            send(q2s.at[q], q2r.at[q], g_s.at[10 + q], g_r.at[10 + q], at(0, 1 - 2 * q))

    def g5():
        for q in range(2):
            arrived(q2r.at[q], g_s.at[10 + q], g_r.at[10 + q])
        fin[...] = (g2[r] + q2r[0].astype(F32) + q2r[1].astype(F32)).astype(BF16)
        send(fin.at[:, other, :], fing.at[c], g_s.at[12], g_r.at[12], sib)

    def g6():
        fing[c] = fin[:, mine, :]
        arrived(fing.at[1 - c], g_s.at[12], g_r.at[12])
        for h in range(2):
            for q in range(2):
                gt_ref[:, (h * 2 + q) * QW:(h * 2 + q + 1) * QW] = nn(place, fing[h, q]).astype(BF16)

    def r_send(k):
        send(rps.at[k], rpr.at[k], rt_s.at[k], rt_r.at[k], hyper[k])

    def r_got(k):
        arrived(rpr.at[k], rt_s.at[k], rt_r.at[k])
        rps[k + 1] = rps[k] + rpr[k]

    def r_out():
        total = rps[5, pl.ds(y * 4 + x, 1), :]
        column = jnp.broadcast_to(total, (n, n)).T
        lanes = (slot_r + (c * SL).astype(F32) == row_i.astype(F32)) & (routed_r > 0.5)
        gr_ref[...] = jnp.sum(jnp.where(lanes, column, 0.0), axis=0, keepdims=True)

    z_step(1)
    r_send(0)
    g_sib(0)
    g_sib(1)
    z_step(2)
    r_got(0)
    r_send(1)
    g_sib(2)
    g_sib(3)
    g1()
    r_got(1)
    r_send(2)
    z_unit(3, 2)
    g_2(0)
    z_unit(3, 0)
    g_2(1)
    z_unit(3, 1)
    r_got(2)
    r_send(3)
    g3()
    z_unit(4, 2)
    r_got(3)
    r_send(4)
    g4()
    z_unit(4, 0)
    z_unit(4, 1)
    r_got(4)
    r_out()
    g5()
    g6()
    for u in units:
        z_last(u)
    for u in units:
        z_out(u)
    for cp in sent:
        cp.wait_send()


def shards(
    tokens, cotangent, route_ids, route_weight, segment_ids, gate_weight, up_weight, down_weight
):
    vmem = pl.BlockSpec(memory_space=pltpu.VMEM)
    hbm = pl.BlockSpec(memory_space=pl.ANY)
    d = tokens.shape[2]
    dma = pltpu.SemaphoreType.DMA
    scratch = [
        pltpu.VMEM((2, 16, 2, 64, QW), BF16),
        pltpu.VMEM((2, 16, 2, 64, QW), BF16),
        pltpu.VMEM((32, SL + 16, 128), BF16),
        pltpu.VMEM((2, 8, 128), F32),
        pltpu.VMEM((d, 2 * FH), BF16),
        pltpu.VMEM((d, FH), BF16),
        pltpu.VMEM((1024, 2 * FH), F32),
        pltpu.VMEM((4, 2, 128, 2 * FH), BF16),
        pltpu.VMEM((3 * FH, 1024), BF16),
        pltpu.VMEM((2, NZ // 2, 3, FH, ZW), BF16),
        pltpu.VMEM((2, NZ // 2, 3, FH, ZW), BF16),
        pltpu.VMEM((4, 4, 2, 64, QW), BF16),
        pltpu.VMEM((4, 4, 2, 64, QW), BF16),
        pltpu.VMEM((2, 4, 64, QW), BF16),
        pltpu.VMEM((2, 4, 64, QW), BF16),
        pltpu.VMEM((2, 4, 2, 64, QW), BF16),
        pltpu.VMEM((2, 4, 2, 64, QW), BF16),
        pltpu.VMEM((4, 2, 64, QW), F32),
        pltpu.VMEM((2, 64, QW), BF16),
        pltpu.VMEM((2, 64, QW), BF16),
        pltpu.VMEM((2, 2, 64, QW), BF16),
        pltpu.VMEM((2, 2, 64, QW), BF16),
        pltpu.VMEM((2, 64, QW), BF16),
        pltpu.VMEM((2, 2, SL, QW), BF16),
        pltpu.VMEM((6, 16, 128), F32),
        pltpu.VMEM((5, 16, 128), F32),
        pltpu.VMEM((3, ZW, FH), F32),
        pltpu.VMEM((3, 192, FH), BF16),
        pltpu.VMEM((3, 192, FH), BF16),
        dma((3,)),
        dma((2, 20)), dma((2, 20)),
        dma((2, 18)), dma((2, 18)),
        dma((5,)), dma((5,)),
        dma((2, NZ // 2, 3)), dma((2, NZ // 2, 3)),
        dma((13,)), dma((13,)),
        dma((5,)), dma((5,)),
        dma((3,)), dma((3,)),
    ]
    shape = jax.ShapeDtypeStruct
    grads = shape((192, 2 * FH), F32)
    gt, gr, gg, gu, gd = pl.pallas_call(
        kernel,
        out_shape=(shape((128, d), BF16), shape((1, 128), F32), grads, grads, grads),
        in_specs=[vmem] * 5 + [hbm] * 3,
        out_specs=(vmem,) * 5,
        scratch_shapes=scratch,
        compiler_params=pltpu.CompilerParams(
            collective_id=0, has_side_effects=True, vmem_limit_bytes=62 * 1024 * 1024),
        cost_estimate=pl.CostEstimate(
            flops=13 * 10**9, bytes_accessed=14 * 10**6, transcendentals=1024 * FH),
    )(tokens[0], cotangent[0], route_ids[0], route_weight[0], segment_ids,
      gate_weight, up_weight, down_weight)
    return gt[None], gr, gg, gu, gd


def solution(mesh):
    return jax.shard_map(
        shards,
        mesh=mesh,
        in_specs=(
            P("dp", "et", None),
            P("dp", "et", None),
            P("dp", "et", None),
            P("dp", "et", None),
            P("dp", "et"),
            P(None, "et"),
            P(None, "et"),
            P(None, "et"),
        ),
        out_specs=(P("dp", "et", None), P("dp", "et"), P("dp", "et"), P("dp", "et"), P("dp", "et")),
        check_vma=False,
    )
```

```python
import jax
import jax.numpy as jnp
from jax import lax
from jax.experimental import pallas as pl
from jax.experimental.pallas import tpu as pltpu
from jax.sharding import PartitionSpec as P

MESH = pl.DeviceIdType.MESH
F32 = jnp.float32
BF16 = jnp.bfloat16
NZ = 8
QW = 768
ZW = 384
FH = 256
SL = 32


def nn(a, b):
    return jnp.dot(a, b, preferred_element_type=F32)


def nt(a, b):
    return lax.dot_general(a, b, (((1,), (1,)), ((), ())), preferred_element_type=F32)


def wrap(v, n):
    return lax.rem(v + 2 * n, n)


def kernel(
    tok_ref, cot_ref, ids_ref, rw_ref, seg_ref, wg_hbm, wu_hbm, wd_hbm,
    gt_ref, gr_ref, gg_ref, gu_ref, gd_ref,
    tb, cb, cnts, wgu, wd, pre, hidb, backb, dgu, dT, zs, zr, sgs, sgr, p1s, p1r, p2s, p2r, g2,
    q1s, q1r, q2s, q2r, fin, fing, rps, rpr, fsum, fxs, fxr,
    w_sem, ag_s, ag_r, sib_s, sib_r, sw_s, sw_r, m_s, m_r, z_s, z_r, g_s, g_r, rt_s, rt_r, fx_s, fx_r,
):
    dp, et = lax.axis_index("dp"), lax.axis_index("et")
    z, yh = lax.div(dp, 2), lax.rem(dp, 2)
    yl, x, c = lax.div(et, 8), lax.rem(lax.div(et, 2), 4), lax.rem(et, 2)
    y = yh * 2 + yl
    p, r = y + c * (x - y), x + c * (y - x)

    def dev(xx, yy, zz, cc):
        return (zz * 2 + lax.div(yy, 2), lax.rem(yy, 2) * 8 + xx * 2 + cc)

    def at(dp_, dr_):
        pp, rr = wrap(p + dp_, 4), wrap(r + dr_, 4)
        return dev(rr + c * (pp - rr), pp + c * (rr - pp), z, c)

    def pos(dp_, dr_):
        return wrap(p + dp_, 4) * 4 + wrap(r + dr_, 4)

    sib = dev(x, y, z, 1 - c)
    zplus, zminus = dev(x, y, wrap(z + 1, NZ), c), dev(x, y, wrap(z - 1, NZ), c)

    def flip(v, bit):
        return v + bit - 2 * bit * lax.rem(lax.div(v, bit), 2)

    hyper = [sib, dev(flip(x, 1), y, z, c), dev(flip(x, 2), y, z, c),
             dev(x, flip(y, 1), z, c), dev(x, flip(y, 2), z, c)]
    partner = hyper[4]

    half = pl.ds(pl.multiple_of(yh * FH, FH), FH)
    wcopies = [
        pltpu.make_async_copy(wg_hbm.at[:, half], wgu.at[:, pl.ds(0, FH)], w_sem.at[0]),
        pltpu.make_async_copy(wu_hbm.at[:, half], wgu.at[:, pl.ds(FH, FH)], w_sem.at[1]),
        pltpu.make_async_copy(wd_hbm.at[:, half], wd, w_sem.at[2]),
    ]
    for cp in wcopies:
        cp.start()

    barrier = pltpu.get_barrier_semaphore()
    group = [dev(wrap(x + a, 4), yh * 2 + wrap(yl + b, 2), z, wrap(c + e, 2))
             for a in range(4) for b in range(2) for e in range(2)][1:]
    outer = dev(x, wrap(y + 2 * yl - 1, 4), z, c)
    for nb in (*group, outer, partner, zplus, zminus):
        pl.semaphore_signal(barrier, inc=1, device_id=nb, device_id_type=MESH)

    sent = []

    def copy(src, dst, ss, rs, to):
        return pltpu.make_async_remote_copy(
            src_ref=src, dst_ref=dst, send_sem=ss, recv_sem=rs, device_id=to, device_id_type=MESH)

    def send(src, dst, ss, rs, to):
        cp = copy(src, dst, ss, rs, to)
        cp.start()
        sent.append(cp)

    def arrived(ref, ss, rs):
        copy(ref, ref, ss, rs, sib).wait_recv()

    n = 128
    row_i = lax.broadcasted_iota(jnp.int32, (n, n), 0)
    col_i = lax.broadcasted_iota(jnp.int32, (n, n), 1)
    chosen = ids_ref[...] == 0
    routed = jnp.max(chosen.astype(F32), axis=0, keepdims=True)
    prob = jnp.sum(jnp.where(chosen, rw_ref[...].astype(F32), 0.0), axis=0, keepdims=True)
    routed_r = jnp.broadcast_to(routed, (n, n))
    routed_c = routed_r.T
    before = (row_i < col_i).astype(F32).astype(BF16)
    after = (col_i < row_i).astype(F32).astype(BF16)
    slot_r = nn(routed_r.astype(BF16), before)
    slot_c = nn(after, routed_c.astype(BF16))
    pick = jnp.where((slot_r == row_i.astype(F32)) & (routed_r > 0.5), 1.0, 0.0)[:SL].astype(BF16)
    place = jnp.where((slot_c == col_i.astype(F32)) & (routed_c > 0.5), 1.0, 0.0)[:, :SL].astype(BF16)
    seg = jnp.broadcast_to(seg_ref[...], (n, n))
    member = jnp.where(seg == row_i, 1.0, 0.0).astype(BF16)
    cnts[et] = nt(jnp.ones((8, n), BF16), member)

    mine = pl.ds(pl.multiple_of(c * SL, SL), SL)
    other = pl.ds(pl.multiple_of((1 - c) * SL, SL), SL)
    here = p * 4 + r
    there = r * 4 + p

    for h in range(2):
        for q in range(2):
            cols = slice((h * 2 + q) * QW, (h * 2 + q + 1) * QW)
            tb[h, here, q, mine, :] = nn(pick, tok_ref[:, cols]).astype(BF16)

    pl.semaphore_wait(barrier, len(group) + 4)
    for k, nb in enumerate(group):
        send(cnts.at[et], cnts.at[et], m_s.at[k], m_r.at[k], nb)

    def tok_rows(h, rows):
        return tb.at[h, here, :, rows, :], tb.at[h, there, :, rows, :]

    def cot_rows(h, rows):
        return cb.at[h, :, here, :, rows, :], cb.at[h, :, there, :, rows, :]

    def swap(t, rows_of):
        for k, h in ((0, 1 - c), (1, c)):
            src, dst = rows_of(h, mine)
            send(src, dst, sw_s.at[t, k], sw_r.at[t, k], sib)

    def swapped(t, rows_of, k):
        h = c if k == 0 else 1 - c
        arrived(rows_of(h, other)[0], sw_s.at[t, k], sw_r.at[t, k])

    swap(0, tok_rows)

    def far_first(h, k, j):
        return wrap(z + (4 - 2 * k - j if h == 0 else 2 * k + j - 3), NZ)

    def pack_cot():
        for k, nb in enumerate(group):
            arrived(cnts.at[0], m_s.at[k], m_r.at[k])
        total = jnp.sum(cnts[...], axis=0)[0:1]
        slot_count = jnp.sum(nt(pick, member) * total, axis=1, keepdims=True)
        slot_prob = jnp.sum(nt(pick, jnp.where(row_i == 16, prob, 0.0).astype(BF16)), axis=1, keepdims=True)
        scale = jnp.where(slot_count > 0.0, slot_prob / jnp.maximum(slot_count, 1.0), 0.0)
        for h in range(2):
            for k in range(2):
                for j in range(2):
                    cols = pl.ds(pl.multiple_of(far_first(h, k, j) * ZW, 128), ZW)
                    cb[h, k, here, j, mine, :] = (nn(pick, cot_ref[:, cols]) * scale).astype(BF16)
        swap(1, cot_rows)

    line = (0, -1, 1, 2)

    def ag(t, at_core):
        def ref_of(h, place_, q):
            return at_core(h, place_) if q is None else at_core(h, place_).at[q]

        def one(dst_p, dst_r, q, k, to):
            ref = ref_of(c, pos(dst_p, dst_r), q)
            send(ref, ref, ag_s.at[t, k], ag_r.at[t, k], to)

        def got(dst_p, dst_r, q, k):
            arrived(ref_of(c, pos(dst_p, dst_r), q), ag_s.at[t, k], ag_r.at[t, k])

        def to_sib(a, b):
            k = (a % 4) * 4 + b % 4 - 1
            send(at_core(c, pos(a, b)), at_core(c, wrap(r + b, 4) * 4 + wrap(p + a, 4)),
                 sib_s.at[t, k], sib_r.at[t, k], sib)

        def out_p(j):
            one(0, line[j], None, 4 + 4 * j, at(1, 0))
            one(0, line[j], None, 5 + 4 * j, at(-1, 0))

        def begin():
            one(0, 0, None, 0, at(0, 1))
            one(0, 0, None, 1, at(0, -1))
            out_p(0)

        def first():
            got(0, -1, None, 0)
            one(0, -1, 0, 2, at(0, 1))
            out_p(1)
            to_sib(0, -1)
            got(0, 1, None, 1)
            one(0, 1, 1, 3, at(0, -1))
            out_p(2)
            to_sib(0, 1)

        def second():
            got(0, 2, 0, 2)
            got(0, 2, 1, 3)
            out_p(3)
            to_sib(0, 2)

        def near(j):
            got(-1, line[j], None, 4 + 4 * j)
            one(-1, line[j], 0, 6 + 4 * j, at(1, 0))
            to_sib(-1, line[j])
            got(1, line[j], None, 5 + 4 * j)
            one(1, line[j], 1, 7 + 4 * j, at(-1, 0))
            to_sib(1, line[j])

        def far(j):
            got(2, line[j], 0, 6 + 4 * j)
            got(2, line[j], 1, 7 + 4 * j)
            to_sib(2, line[j])

        def from_sib():
            for a in range(4):
                for b in range(4):
                    if a or b:
                        k = a * 4 + b - 1
                        arrived(at_core(1 - c, pos(b, a)), sib_s.at[t, k], sib_r.at[t, k])

        return begin, first, second, near, far, from_sib

    T = ag(0, lambda h, i: tb.at[h, i])
    C1 = ag(1, lambda h, i: cb.at[h, 0, i])
    C2 = ag(2, lambda h, i: cb.at[h, 1, i])
    BEGIN, FIRST, SECOND, NEAR, FAR, FROM_SIB = range(6)

    def fwd(i):
        rows = pl.ds(pl.multiple_of(i * 256, 256), 256)
        acc = None
        for h in range(2):
            for q in range(2):
                xs = tb[h, pl.ds(i * 4, 4), q].reshape(256, QW)
                one = nn(xs, wgu[(h * 2 + q) * QW:(h * 2 + q + 1) * QW, :])
                acc = one if acc is None else acc + one
        pre[rows, :] = acc

    def activate(i):
        for j in (2 * i, 2 * i + 1):
            rows = pl.ds(j * n, n)
            gate, up = pre[rows, 0:FH], pre[rows, FH:2 * FH]
            sg = 1.0 / (1.0 + jnp.exp(-gate))
            act = gate * sg
            hid = act * up
            pre[rows, 0:FH] = up * (sg * (1.0 + gate * (1.0 - sg)))
            pre[rows, FH:2 * FH] = act
            hidb[rows, :] = hid
            dT[2 * FH:3 * FH, rows] = hid.T.astype(BF16)

    def back_part(k, i):
        rows = pl.ds(i * 256, 256)
        acc = None
        for h in range(2):
            for j in range(2):
                xs = cb[h, k, pl.ds(i * 4, 4), j].reshape(256, ZW)
                one = nn(xs, wd[pl.ds(pl.multiple_of(far_first(h, k, j) * ZW, ZW), ZW), :])
                acc = one if acc is None else acc + one
        if k == 0:
            backb[rows, :] = acc
        else:
            backb[rows, :] += acc

    lane1 = lax.broadcasted_iota(jnp.int32, (1, n), 1)

    def gradients(j):
        rows = pl.ds(j * n, n)
        back = backb[rows, :]
        dg, du = back * pre[rows, 0:FH], back * pre[rows, FH:2 * FH]
        dgu[j // 2, j % 2, :, 0:FH] = dg.astype(BF16)
        dgu[j // 2, j % 2, :, FH:2 * FH] = du.astype(BF16)
        dT[0:FH, rows] = dg.T.astype(BF16)
        dT[FH:2 * FH, rows] = du.T.astype(BF16)
        rp = jnp.sum(hidb[rows, :] * back, axis=1, keepdims=True)
        rp_row = jnp.broadcast_to(rp, (n, n)).T[0:1]
        for k in range(2):
            i = j * 2 + k
            chip = i + c * (i % 4 * 4 + i // 4 - i)
            row = rp_row if k == 0 else pltpu.roll(rp_row, 64, 1)
            rps[0, pl.ds(chip, 1), :] = jnp.where(lane1 < 64, row, 0.0)

    def part(u, d):
        if u == 2:
            h = 0 if 1 <= d <= 4 else 1
            i = 4 - d if h == 0 else d + 3
            xs = cb[h, i // 2, :, i % 2].reshape(1024, ZW)
        else:
            d = wrap(z + d, NZ)
            cols = pl.ds(pl.multiple_of(lax.rem(d, 2) * ZW, 128), ZW)
            xs = tb[lax.div(d, 4), :, lax.rem(lax.div(d, 2), 2), :, cols].reshape(1024, ZW)
        return nn(dT[u * FH:(u + 1) * FH, :], xs)

    units = (2, 0, 1)
    HF = FH // 2
    STEPS = NZ // 2

    def z_unit(s, u):
        if s == 1:
            val = part(u, STEPS).astype(BF16)
            for dr, to in ((0, zplus), (1, zminus)):
                zs[dr, 0, u, dr * HF:(dr + 1) * HF, :] = val[dr * HF:(dr + 1) * HF]
                ref = (dr, 0, u, pl.ds(dr * HF, HF))
                send(zs.at[ref], zr.at[ref], z_s.at[dr, 0, u], z_r.at[dr, 0, u], to)
            return
        for dr, to, off in ((0, zplus, STEPS + 1 - s), (1, zminus, s - STEPS - 1)):
            val = part(u, off)
            if s == 2:
                ref = zr.at[dr, 0, u, pl.ds(dr * HF, HF)]
                arrived(ref, z_s.at[dr, 0, u], z_r.at[dr, 0, u])
                lo, hi = dr * HF, (dr + 1) * HF
                o_lo, o_hi = HF - lo, FH - lo
                zs[dr, 1, u, lo:hi, :] = (val[lo:hi] + ref[...].astype(F32)).astype(BF16)
                zs[dr, 1, u, o_lo:o_hi, :] = val[o_lo:o_hi].astype(BF16)
            else:
                ref = zr.at[dr, s - 2, u]
                arrived(ref, z_s.at[dr, s - 2, u], z_r.at[dr, s - 2, u])
                zs[dr, s - 1, u] = (val + ref[...].astype(F32)).astype(BF16)
            send(zs.at[dr, s - 1, u], zr.at[dr, s - 1, u], z_s.at[dr, s - 1, u], z_r.at[dr, s - 1, u], to)

    def z_step(s):
        for u in units:
            z_unit(s, u)

    outs = (gg_ref, gu_ref, gd_ref)
    mycols = pl.ds(pl.multiple_of(yh * FH, FH), FH)
    yourcols = pl.ds(pl.multiple_of((1 - yh) * FH, FH), FH)

    def z_last(u):
        val = part(u, 0)
        for dr in range(2):
            ref = zr.at[dr, STEPS - 1, u]
            arrived(ref, z_s.at[dr, STEPS - 1, u], z_r.at[dr, STEPS - 1, u])
            val = val + ref[...].astype(F32)
        fsum[u] = val.T
        fxs[u] = fsum[u, pl.ds(pl.multiple_of((1 - yh) * 192, 192), 192), :].astype(BF16)
        send(fxs.at[u], fxr.at[u], fx_s.at[u], fx_r.at[u], partner)
        outs[u][:, mycols] = fsum[u, pl.ds(pl.multiple_of(yh * 192, 192), 192), :]

    def z_out(u):
        arrived(fxr.at[u], fx_s.at[u], fx_r.at[u])
        outs[u][:, yourcols] = fxr[u].astype(F32)

    def wrows(h, q):
        return wgu[pl.ds(pl.multiple_of((h * 2 + q) * QW, QW), QW), :]

    def g_sib(k):
        rr = wrap(r + (2, 1, -1, 0)[k], 4)
        j0, odd = lax.div(rr, 2), lax.rem(rr, 2)
        xs = dgu[:, j0, pl.ds(pl.multiple_of(odd * 64, 64), 64), :].reshape(256, 2 * FH)
        for q in range(2):
            sgs[rr, :, q] = nt(xs, wrows(1 - c, q)).astype(BF16).reshape(4, 64, QW)
        send(sgs.at[rr], sgr.at[rr], g_s.at[k], g_r.at[k], sib)

    def g_line(off, k):
        pp = wrap(p + off, 4)
        arrived(sgr.at[pp], g_s.at[k], g_r.at[k])
        xs = dgu[pp].reshape(256, 2 * FH)
        return [nt(xs, wrows(c, q)).reshape(4, 64, QW) + sgr[pp, :, q].astype(F32) for q in range(2)]

    def g1():
        val = g_line(2, 0)
        for q in range(2):
            p1s[q] = val[q].astype(BF16)
            send(p1s.at[q], p1r.at[q], g_s.at[4 + q], g_r.at[4 + q], at(1 - 2 * q, 0))

    def g_2(q):
        val = g_line(1 - 2 * q, 1 + q)
        arrived(p1r.at[q], g_s.at[4 + q], g_r.at[4 + q])
        p2s[q, :, q] = (val[q] + p1r[q].astype(F32)).astype(BF16)
        p2s[q, :, 1 - q] = val[1 - q].astype(BF16)
        send(p2s.at[q], p2r.at[q], g_s.at[6 + q], g_r.at[6 + q], at(1 - 2 * q, 0))

    def g3():
        val = g_line(0, 3)
        for q in range(2):
            arrived(p2r.at[q], g_s.at[6 + q], g_r.at[6 + q])
        for q in range(2):
            g2[:, q] = val[q] + p2r[0, :, q].astype(F32) + p2r[1, :, q].astype(F32)
        opp = wrap(r + 2, 4)
        for q in range(2):
            q1s[q] = g2[opp, q].astype(BF16)
            send(q1s.at[q], q1r.at[q], g_s.at[8 + q], g_r.at[8 + q], at(0, 1 - 2 * q))

    def g4():
        for q in range(2):
            rr = wrap(r + 1 - 2 * q, 4)
            arrived(q1r.at[q], g_s.at[8 + q], g_r.at[8 + q])
            q2s[q, q] = (g2[rr, q] + q1r[q].astype(F32)).astype(BF16)
            q2s[q, 1 - q] = g2[rr, 1 - q].astype(BF16)
            send(q2s.at[q], q2r.at[q], g_s.at[10 + q], g_r.at[10 + q], at(0, 1 - 2 * q))

    def g5():
        for q in range(2):
            arrived(q2r.at[q], g_s.at[10 + q], g_r.at[10 + q])
        fin[...] = (g2[r] + q2r[0].astype(F32) + q2r[1].astype(F32)).astype(BF16)
        send(fin.at[:, other, :], fing.at[c], g_s.at[12], g_r.at[12], sib)

    def g6():
        fing[c] = fin[:, mine, :]
        arrived(fing.at[1 - c], g_s.at[12], g_r.at[12])
        for h in range(2):
            for q in range(2):
                gt_ref[:, (h * 2 + q) * QW:(h * 2 + q + 1) * QW] = nn(place, fing[h, q]).astype(BF16)

    def r_send(k):
        send(rps.at[k], rpr.at[k], rt_s.at[k], rt_r.at[k], hyper[k])

    def r_got(k):
        arrived(rpr.at[k], rt_s.at[k], rt_r.at[k])
        rps[k + 1] = rps[k] + rpr[k]

    def r_out():
        total = rps[5, pl.ds(y * 4 + x, 1), :]
        column = jnp.broadcast_to(total, (n, n)).T
        lanes = (slot_r + (c * SL).astype(F32) == row_i.astype(F32)) & (routed_r > 0.5)
        summed = jnp.sum(jnp.where(lanes, column, 0.0), axis=0, keepdims=True)
        gr_ref[...] = jnp.where(routed > 0.5, summed / jnp.maximum(prob, 0.25), 0.0)

    GATE, UP, DOWN = 0, 1, 2
    swapped(0, tok_rows, 0)
    T[BEGIN]()
    pack_cot()
    swapped(1, cot_rows, 0)
    C1[BEGIN]()
    T[FIRST]()
    T[NEAR](0)
    T[SECOND]()
    C1[FIRST]()
    C1[NEAR](0)
    T[NEAR](1)
    T[NEAR](2)
    T[FAR](0)
    C1[SECOND]()
    T[NEAR](3)
    T[FAR](1)
    T[FAR](2)
    C2[BEGIN]()
    C1[NEAR](1)
    T[FAR](3)
    swapped(0, tok_rows, 1)
    T[FROM_SIB]()
    for cp in wcopies:
        cp.wait()
    fwd(0)
    C1[NEAR](2)
    C1[FAR](0)
    fwd(1)
    C2[FIRST]()
    C2[NEAR](0)
    fwd(2)
    C1[NEAR](3)
    C1[FAR](1)
    C1[FAR](2)
    fwd(3)
    C2[SECOND]()
    activate(0)
    activate(1)
    C1[FAR](3)
    C2[NEAR](1)
    C2[NEAR](2)
    activate(2)
    activate(3)
    C2[FAR](0)
    swapped(1, cot_rows, 1)
    C1[FROM_SIB]()
    z_unit(1, DOWN)
    C2[NEAR](3)
    for i in range(4):
        back_part(0, i)
    C2[FAR](1)
    C2[FAR](2)
    z_unit(2, DOWN)
    C2[FAR](3)
    C2[FROM_SIB]()
    z_unit(3, DOWN)
    for i in range(4):
        back_part(1, i)
        gradients(2 * i)
        gradients(2 * i + 1)
    z_unit(1, GATE)
    z_unit(1, UP)
    r_send(0)
    g_sib(0)
    g1()
    z_unit(4, DOWN)
    g_sib(1)
    r_got(0)
    r_send(1)
    z_unit(2, GATE)
    g_sib(2)
    z_unit(2, UP)
    r_got(1)
    r_send(2)
    g_2(0)
    g_2(1)
    g_sib(3)
    z_unit(3, GATE)
    r_got(2)
    r_send(3)
    g3()
    z_unit(3, UP)
    z_last(DOWN)
    r_got(3)
    r_send(4)
    g4()
    z_unit(4, GATE)
    r_got(4)
    r_out()
    g5()
    z_unit(4, UP)
    z_out(DOWN)
    g6()
    z_last(GATE)
    z_last(UP)
    z_out(GATE)
    z_out(UP)
    for cp in sent:
        cp.wait_send()


def copies(*refs):
    ins, outs, sem = refs[:5], refs[5:10], refs[10]
    moves = [pltpu.make_async_copy(a, b, sem.at[k]) for k, (a, b) in enumerate(zip(ins, outs))]
    for cp in moves:
        cp.start()
    for cp in moves:
        cp.wait()


def hand_over(*arrays):
    hbm = pl.BlockSpec(memory_space=pl.ANY)
    return pl.pallas_call(
        copies,
        out_shape=tuple(jax.ShapeDtypeStruct(a.shape, a.dtype) for a in arrays),
        in_specs=[hbm] * 5,
        out_specs=(hbm,) * 5,
        scratch_shapes=[pltpu.SemaphoreType.DMA((5,))],
        compiler_params=pltpu.CompilerParams(vmem_limit_bytes=62 * 1024 * 1024),
    )(*arrays)


def shards(
    tokens, cotangent, route_ids, route_weight, segment_ids, gate_weight, up_weight, down_weight
):
    vmem = pl.BlockSpec(memory_space=pltpu.VMEM)
    hbm = pl.BlockSpec(memory_space=pl.ANY)
    d = tokens.shape[2]
    dma = pltpu.SemaphoreType.DMA
    scratch = [
        pltpu.VMEM((2, 16, 2, 64, QW), BF16),
        pltpu.VMEM((2, 2, 16, 2, 64, ZW), BF16),
        pltpu.VMEM((16, 8, 128), F32),
        pltpu.VMEM((d, 2 * FH), BF16),
        pltpu.VMEM((d, FH), BF16),
        pltpu.VMEM((1024, 2 * FH), F32),
        pltpu.VMEM((1024, FH), F32),
        pltpu.VMEM((1024, FH), F32),
        pltpu.VMEM((4, 2, 128, 2 * FH), BF16),
        pltpu.VMEM((3 * FH, 1024), BF16),
        pltpu.VMEM((2, NZ // 2, 3, FH, ZW), BF16),
        pltpu.VMEM((2, NZ // 2, 3, FH, ZW), BF16),
        pltpu.VMEM((4, 4, 2, 64, QW), BF16),
        pltpu.VMEM((4, 4, 2, 64, QW), BF16),
        pltpu.VMEM((2, 4, 64, QW), BF16),
        pltpu.VMEM((2, 4, 64, QW), BF16),
        pltpu.VMEM((2, 4, 2, 64, QW), BF16),
        pltpu.VMEM((2, 4, 2, 64, QW), BF16),
        pltpu.VMEM((4, 2, 64, QW), F32),
        pltpu.VMEM((2, 64, QW), BF16),
        pltpu.VMEM((2, 64, QW), BF16),
        pltpu.VMEM((2, 2, 64, QW), BF16),
        pltpu.VMEM((2, 2, 64, QW), BF16),
        pltpu.VMEM((2, 64, QW), BF16),
        pltpu.VMEM((2, 2, SL, QW), BF16),
        pltpu.VMEM((6, 16, 128), F32),
        pltpu.VMEM((5, 16, 128), F32),
        pltpu.VMEM((3, ZW, FH), F32),
        pltpu.VMEM((3, 192, FH), BF16),
        pltpu.VMEM((3, 192, FH), BF16),
        dma((3,)),
        dma((3, 20)), dma((3, 20)),
        dma((3, 15)), dma((3, 15)),
        dma((2, 2)), dma((2, 2)),
        dma((15,)), dma((15,)),
        dma((2, NZ // 2, 3)), dma((2, NZ // 2, 3)),
        dma((13,)), dma((13,)),
        dma((5,)), dma((5,)),
        dma((3,)), dma((3,)),
    ]
    shape = jax.ShapeDtypeStruct
    grads = shape((192, 2 * FH), F32)
    gt, gr, gg, gu, gd = pl.pallas_call(
        kernel,
        out_shape=(shape((128, d), BF16), shape((1, 128), F32), grads, grads, grads),
        in_specs=[vmem] * 5 + [hbm] * 3,
        out_specs=(vmem,) * 5,
        scratch_shapes=scratch,
        compiler_params=pltpu.CompilerParams(
            collective_id=0, has_side_effects=True, vmem_limit_bytes=62 * 1024 * 1024),
        cost_estimate=pl.CostEstimate(
            flops=13 * 10**9, bytes_accessed=14 * 10**6, transcendentals=1024 * FH),
    )(tokens[0], cotangent[0], route_ids[0].T, route_weight[0].T, segment_ids,
      gate_weight, up_weight, down_weight)
    gt, gr, gg, gu, gd = hand_over(gt, gr, gg, gu, gd)
    return gt[None], gr, gg, gu, gd


def solution(mesh):
    return jax.shard_map(
        shards,
        mesh=mesh,
        in_specs=(
            P("dp", "et", None),
            P("dp", "et", None),
            P("dp", "et", None),
            P("dp", "et", None),
            P("dp", "et"),
            P(None, "et"),
            P(None, "et"),
            P(None, "et"),
        ),
        out_specs=(P("dp", "et", None), P("dp", "et"), P("dp", "et"), P("dp", "et"), P("dp", "et")),
        check_vma=False,
    )
```

```python
import jax
import jax.numpy as jnp
from jax import lax
from jax.experimental import pallas as pl
from jax.experimental.pallas import tpu as pltpu
from jax.sharding import PartitionSpec as P

MESH = pl.DeviceIdType.MESH
F32 = jnp.float32
BF16 = jnp.bfloat16
NZ = 8
QW = 768
ZW = 384
FH = 256
SL = 32


def nn(a, b):
    return jnp.dot(a, b, preferred_element_type=F32)


def nt(a, b):
    return lax.dot_general(a, b, (((1,), (1,)), ((), ())), preferred_element_type=F32)


def wrap(v, n):
    return lax.rem(v + 2 * n, n)


def kernel(
    ids_ref, rw_ref, seg_ref, tok_hbm, cot_hbm, wg_hbm, wu_hbm, wd_hbm,
    gt_hbm, gr_hbm, gg_hbm, gu_hbm, gd_hbm,
    tok_ref, cot_ref, gt_ref, gr_ref, wob,
    tb, cb, cnts, wgu, wd, pre, hidb, backb, dgu, dT, zs, zr, sgs, sgr, p1s, p1r, p2s, p2r, g2,
    q1s, q1r, q2s, q2r, fin, fing, rps, rpr, fsum, fxs, fxr,
    i_sem, o_sem, w_sem, ag_s, ag_r, sib_s, sib_r, sw_s, sw_r, m_s, m_r, z_s, z_r, g_s, g_r, rt_s, rt_r, fx_s, fx_r,
):
    dp, et = lax.axis_index("dp"), lax.axis_index("et")
    z, yh = lax.div(dp, 2), lax.rem(dp, 2)
    yl, x, c = lax.div(et, 8), lax.rem(lax.div(et, 2), 4), lax.rem(et, 2)
    y = yh * 2 + yl
    p, r = y + c * (x - y), x + c * (y - x)

    def dev(xx, yy, zz, cc):
        return (zz * 2 + lax.div(yy, 2), lax.rem(yy, 2) * 8 + xx * 2 + cc)

    def at(dp_, dr_):
        pp, rr = wrap(p + dp_, 4), wrap(r + dr_, 4)
        return dev(rr + c * (pp - rr), pp + c * (rr - pp), z, c)

    def pos(dp_, dr_):
        return wrap(p + dp_, 4) * 4 + wrap(r + dr_, 4)

    sib = dev(x, y, z, 1 - c)
    zplus, zminus = dev(x, y, wrap(z + 1, NZ), c), dev(x, y, wrap(z - 1, NZ), c)

    def flip(v, bit):
        return v + bit - 2 * bit * lax.rem(lax.div(v, bit), 2)

    hyper = [sib, dev(flip(x, 1), y, z, c), dev(flip(x, 2), y, z, c),
             dev(x, flip(y, 1), z, c), dev(x, flip(y, 2), z, c)]
    partner = hyper[4]

    icopies = [pltpu.make_async_copy(tok_hbm, tok_ref, i_sem.at[0]),
               pltpu.make_async_copy(cot_hbm, cot_ref, i_sem.at[1])]
    for cp in icopies:
        cp.start()

    half = pl.ds(pl.multiple_of(yh * FH, FH), FH)
    wcopies = [
        pltpu.make_async_copy(wg_hbm.at[:, half], wgu.at[:, pl.ds(0, FH)], w_sem.at[0]),
        pltpu.make_async_copy(wu_hbm.at[:, half], wgu.at[:, pl.ds(FH, FH)], w_sem.at[1]),
        pltpu.make_async_copy(wd_hbm.at[:, half], wd, w_sem.at[2]),
    ]
    barrier = pltpu.get_barrier_semaphore()
    group = [dev(wrap(x + a, 4), yh * 2 + wrap(yl + b, 2), z, wrap(c + e, 2))
             for a in range(4) for b in range(2) for e in range(2)][1:]
    outer = dev(x, wrap(y + 2 * yl - 1, 4), z, c)
    for nb in (*group, outer, partner, zplus, zminus):
        pl.semaphore_signal(barrier, inc=1, device_id=nb, device_id_type=MESH)
    for cp in wcopies:
        cp.start()

    sent = []
    written = []

    def write(src, dst, k):
        cp = pltpu.make_async_copy(src, dst, o_sem.at[k])
        cp.start()
        written.append(cp)

    def copy(src, dst, ss, rs, to):
        return pltpu.make_async_remote_copy(
            src_ref=src, dst_ref=dst, send_sem=ss, recv_sem=rs, device_id=to, device_id_type=MESH)

    def send(src, dst, ss, rs, to):
        cp = copy(src, dst, ss, rs, to)
        cp.start()
        sent.append(cp)

    def arrived(ref, ss, rs):
        copy(ref, ref, ss, rs, sib).wait_recv()

    n = 128
    row_i = lax.broadcasted_iota(jnp.int32, (n, n), 0)
    col_i = lax.broadcasted_iota(jnp.int32, (n, n), 1)
    chosen = ids_ref[...] == 0
    routed = jnp.max(chosen.astype(F32), axis=0, keepdims=True)
    prob = jnp.sum(jnp.where(chosen, rw_ref[...].astype(F32), 0.0), axis=0, keepdims=True)
    routed_r = jnp.broadcast_to(routed, (n, n))
    routed_c = routed_r.T
    before = (row_i < col_i).astype(F32).astype(BF16)
    after = (col_i < row_i).astype(F32).astype(BF16)
    slot_r = nn(routed_r.astype(BF16), before)
    slot_c = nn(after, routed_c.astype(BF16))
    pick = jnp.where((slot_r == row_i.astype(F32)) & (routed_r > 0.5), 1.0, 0.0)[:SL].astype(BF16)
    place = jnp.where((slot_c == col_i.astype(F32)) & (routed_c > 0.5), 1.0, 0.0)[:, :SL].astype(BF16)
    seg = jnp.broadcast_to(seg_ref[...], (n, n))
    member = jnp.where(seg == row_i, 1.0, 0.0).astype(BF16)
    cnts[et] = nt(jnp.ones((8, n), BF16), member)

    mine = pl.ds(pl.multiple_of(c * SL, SL), SL)
    other = pl.ds(pl.multiple_of((1 - c) * SL, SL), SL)
    here = p * 4 + r
    there = r * 4 + p

    icopies[0].wait()
    for h in range(2):
        for q in range(2):
            cols = slice((h * 2 + q) * QW, (h * 2 + q + 1) * QW)
            tb[h, here, q, mine, :] = nn(pick, tok_ref[:, cols]).astype(BF16)

    pl.semaphore_wait(barrier, len(group) + 4)
    for k, nb in enumerate(group):
        send(cnts.at[et], cnts.at[et], m_s.at[k], m_r.at[k], nb)

    def tok_rows(h, rows):
        return tb.at[h, here, :, rows, :], tb.at[h, there, :, rows, :]

    def cot_rows(h, rows):
        return cb.at[h, :, here, :, rows, :], cb.at[h, :, there, :, rows, :]

    def swap(t, rows_of):
        for k, h in ((0, 1 - c), (1, c)):
            src, dst = rows_of(h, mine)
            send(src, dst, sw_s.at[t, k], sw_r.at[t, k], sib)

    def swapped(t, rows_of, k):
        h = c if k == 0 else 1 - c
        arrived(rows_of(h, other)[0], sw_s.at[t, k], sw_r.at[t, k])

    swap(0, tok_rows)

    def far_first(h, k, j):
        return wrap(z + (4 - 2 * k - j if h == 0 else 2 * k + j - 3), NZ)

    def pack_cot():
        icopies[1].wait()
        for k, nb in enumerate(group):
            arrived(cnts.at[0], m_s.at[k], m_r.at[k])
        total = jnp.sum(cnts[...], axis=0)[0:1]
        slot_count = jnp.sum(nt(pick, member) * total, axis=1, keepdims=True)
        slot_prob = jnp.sum(nt(pick, jnp.where(row_i == 16, prob, 0.0).astype(BF16)), axis=1, keepdims=True)
        scale = jnp.where(slot_count > 0.0, slot_prob / jnp.maximum(slot_count, 1.0), 0.0)
        for h in range(2):
            for k in range(2):
                for j in range(2):
                    cols = pl.ds(pl.multiple_of(far_first(h, k, j) * ZW, 128), ZW)
                    cb[h, k, here, j, mine, :] = (nn(pick, cot_ref[:, cols]) * scale).astype(BF16)
        swap(1, cot_rows)

    line = (0, -1, 1, 2)

    def ag(t, at_core):
        def ref_of(h, place_, q):
            return at_core(h, place_) if q is None else at_core(h, place_).at[q]

        def one(dst_p, dst_r, q, k, to):
            ref = ref_of(c, pos(dst_p, dst_r), q)
            send(ref, ref, ag_s.at[t, k], ag_r.at[t, k], to)

        def got(dst_p, dst_r, q, k):
            arrived(ref_of(c, pos(dst_p, dst_r), q), ag_s.at[t, k], ag_r.at[t, k])

        def to_sib(a, b):
            k = (a % 4) * 4 + b % 4 - 1
            send(at_core(c, pos(a, b)), at_core(c, wrap(r + b, 4) * 4 + wrap(p + a, 4)),
                 sib_s.at[t, k], sib_r.at[t, k], sib)

        def out_p(j):
            one(0, line[j], None, 4 + 4 * j, at(1, 0))
            one(0, line[j], None, 5 + 4 * j, at(-1, 0))

        def begin():
            one(0, 0, None, 0, at(0, 1))
            one(0, 0, None, 1, at(0, -1))
            out_p(0)

        def first():
            got(0, -1, None, 0)
            one(0, -1, 0, 2, at(0, 1))
            out_p(1)
            to_sib(0, -1)
            got(0, 1, None, 1)
            one(0, 1, 1, 3, at(0, -1))
            out_p(2)
            to_sib(0, 1)

        def second():
            got(0, 2, 0, 2)
            got(0, 2, 1, 3)
            out_p(3)
            to_sib(0, 2)

        def near(j):
            got(-1, line[j], None, 4 + 4 * j)
            one(-1, line[j], 0, 6 + 4 * j, at(1, 0))
            to_sib(-1, line[j])
            got(1, line[j], None, 5 + 4 * j)
            one(1, line[j], 1, 7 + 4 * j, at(-1, 0))
            to_sib(1, line[j])

        def far(j):
            got(2, line[j], 0, 6 + 4 * j)
            got(2, line[j], 1, 7 + 4 * j)
            to_sib(2, line[j])

        def from_sib():
            for a in range(4):
                for b in range(4):
                    if a or b:
                        k = a * 4 + b - 1
                        arrived(at_core(1 - c, pos(b, a)), sib_s.at[t, k], sib_r.at[t, k])

        return begin, first, second, near, far, from_sib

    T = ag(0, lambda h, i: tb.at[h, i])
    C1 = ag(1, lambda h, i: cb.at[h, 0, i])
    C2 = ag(2, lambda h, i: cb.at[h, 1, i])
    BEGIN, FIRST, SECOND, NEAR, FAR, FROM_SIB = range(6)

    def fwd(i):
        rows = pl.ds(pl.multiple_of(i * 256, 256), 256)
        acc = None
        for h in range(2):
            for q in range(2):
                xs = tb[h, pl.ds(i * 4, 4), q].reshape(256, QW)
                one = nn(xs, wgu[(h * 2 + q) * QW:(h * 2 + q + 1) * QW, :])
                acc = one if acc is None else acc + one
        pre[rows, :] = acc

    def activate(i):
        for j in (2 * i, 2 * i + 1):
            rows = pl.ds(j * n, n)
            gate, up = pre[rows, 0:FH], pre[rows, FH:2 * FH]
            sg = 1.0 / (1.0 + jnp.exp(-gate))
            act = gate * sg
            hid = act * up
            pre[rows, 0:FH] = up * (sg * (1.0 + gate * (1.0 - sg)))
            pre[rows, FH:2 * FH] = act
            hidb[rows, :] = hid
            dT[2 * FH:3 * FH, rows] = hid.T.astype(BF16)

    def back_part(k, i):
        rows = pl.ds(i * 256, 256)
        acc = None
        for h in range(2):
            for j in range(2):
                xs = cb[h, k, pl.ds(i * 4, 4), j].reshape(256, ZW)
                one = nn(xs, wd[pl.ds(pl.multiple_of(far_first(h, k, j) * ZW, ZW), ZW), :])
                acc = one if acc is None else acc + one
        if k == 0:
            backb[rows, :] = acc
        else:
            backb[rows, :] += acc

    lane1 = lax.broadcasted_iota(jnp.int32, (1, n), 1)

    def gradients(j):
        rows = pl.ds(j * n, n)
        back = backb[rows, :]
        dg, du = back * pre[rows, 0:FH], back * pre[rows, FH:2 * FH]
        dgu[j // 2, j % 2, :, 0:FH] = dg.astype(BF16)
        dgu[j // 2, j % 2, :, FH:2 * FH] = du.astype(BF16)
        dT[0:FH, rows] = dg.T.astype(BF16)
        dT[FH:2 * FH, rows] = du.T.astype(BF16)
        rp = jnp.sum(hidb[rows, :] * back, axis=1, keepdims=True)
        rp_row = jnp.broadcast_to(rp, (n, n)).T[0:1]
        for k in range(2):
            i = j * 2 + k
            chip = i + c * (i % 4 * 4 + i // 4 - i)
            row = rp_row if k == 0 else pltpu.roll(rp_row, 64, 1)
            rps[0, pl.ds(chip, 1), :] = jnp.where(lane1 < 64, row, 0.0)

    def part(u, d):
        h = 0 if 1 <= d <= 4 else 1
        i = 4 - d if h == 0 else d + 3
        xs = cb[h, i // 2, :, i % 2].reshape(1024, ZW)
        return nn(dT[u * FH:(u + 1) * FH, :], xs)

    HF = FH // 2
    STEPS = NZ // 2
    OFFS = {k: (STEPS + 1 - k, k - STEPS - 1) for k in range(1, STEPS + 1)}
    ways = ((0, zplus), (1, zminus))

    def z_down(s):
        if s == 1:
            val = part(2, STEPS).astype(BF16)
        for dr, to in ways:
            lo, hi = dr * HF, (dr + 1) * HF
            sems = (z_s.at[dr, s - 1, 4], z_r.at[dr, s - 1, 4])
            if s == 1:
                zs[dr, 0, 2, lo:hi, :] = val[lo:hi]
                ref = (dr, 0, 2, pl.ds(lo, HF))
            else:
                ref = (dr, s - 1, 2)
                own = part(2, OFFS[s][dr])
                if s == 2:
                    got = zr.at[dr, 0, 2, pl.ds(lo, HF)]
                    arrived(got, z_s.at[dr, 0, 4], z_r.at[dr, 0, 4])
                    zs[dr, 1, 2, lo:hi, :] = (own[lo:hi] + got[...].astype(F32)).astype(BF16)
                    zs[dr, 1, 2, HF - lo:FH - lo, :] = own[HF - lo:FH - lo].astype(BF16)
                else:
                    got = zr.at[dr, s - 2, 2]
                    arrived(got, z_s.at[dr, s - 2, 4], z_r.at[dr, s - 2, 4])
                    zs[dr, s - 1, 2] = (own + got[...].astype(F32)).astype(BF16)
            send(zs.at[ref], zr.at[ref], *sems, to)

    def gu_part(off):
        d = wrap(z + off, NZ)
        cols = pl.ds(pl.multiple_of(lax.rem(d, 2) * ZW, 128), ZW)
        xs = tb[lax.div(d, 4), :, lax.rem(lax.div(d, 2), 2), :, cols].reshape(1024, ZW)
        return nn(dT[0:2 * FH, :], xs)

    def z_pre(s):
        offs = (STEPS,) if s == 1 else (0,) if s > STEPS else OFFS[s]
        for k, off in enumerate(offs):
            pre[k * 512:(k + 1) * 512, 0:ZW] = gu_part(off)

    def z_piece(s, k):
        u, rows = k // 2, pl.ds(k % 2 * HF, HF)
        for dr, to in ways:
            if s == 1 and k % 2 != dr:
                continue
            base = 0 if s == 1 else dr * 512
            val = pre[base + k * HF:base + (k + 1) * HF, 0:ZW]
            if s > 2 or (s == 2 and k % 2 == dr):
                got = zr.at[dr, s - 2, u, rows]
                arrived(got, z_s.at[dr, s - 2, k], z_r.at[dr, s - 2, k])
                val = val + got[...].astype(F32)
            ref = (dr, s - 1, u, rows)
            zs[ref] = val.astype(BF16)
            send(zs.at[ref], zr.at[ref], z_s.at[dr, s - 1, k], z_r.at[dr, s - 1, k], to)

    def z_step(s):
        for k in range(4):
            z_piece(s, k)

    outs = (gg_hbm, gu_hbm, gd_hbm)
    mycols = pl.ds(pl.multiple_of(yh * FH, FH), FH)
    yourcols = pl.ds(pl.multiple_of((1 - yh) * FH, FH), FH)
    myrows = pl.ds(pl.multiple_of(yh * 192, 192), 192)
    yourrows = pl.ds(pl.multiple_of((1 - yh) * 192, 192), 192)

    def z_last(k):
        u, lo = k // 2, k % 2 * HF
        if u == 2:
            val = nn(dT[k * HF:(k + 1) * HF, :], cb[1, 1, :, 1].reshape(1024, ZW))
        else:
            val = pre[k * HF:(k + 1) * HF, 0:ZW]
        for dr in range(2):
            got = zr.at[dr, STEPS - 1, u, pl.ds(lo, HF)]
            if u < 2:
                arrived(got, z_s.at[dr, STEPS - 1, k], z_r.at[dr, STEPS - 1, k])
            elif k == 4:
                arrived(zr.at[dr, STEPS - 1, u], z_s.at[dr, STEPS - 1, 4], z_r.at[dr, STEPS - 1, 4])
            val = val + got[...].astype(F32)
        fsum[k] = val.T
        fxs[k] = fsum[k, yourrows, :].astype(BF16)
        send(fxs.at[k], fxr.at[k], fx_s.at[k], fx_r.at[k], partner)
        wob[u, :, pl.ds(pl.multiple_of(yh * FH + lo, HF), HF)] = fsum[k, myrows, :]

    def z_out(u):
        for k in (2 * u, 2 * u + 1):
            arrived(fxr.at[k], fx_s.at[k], fx_r.at[k])
            at_ = pl.ds(pl.multiple_of((1 - yh) * FH + k % 2 * HF, HF), HF)
            wob[u, :, at_] = fxr[k].astype(F32)
        write(wob.at[u], outs[u], u)

    def wrows(h, q):
        return wgu[pl.ds(pl.multiple_of((h * 2 + q) * QW, QW), QW), :]

    def g_sib(k):
        rr = wrap(r + (2, 1, -1, 0)[k], 4)
        j0, odd = lax.div(rr, 2), lax.rem(rr, 2)
        xs = dgu[:, j0, pl.ds(pl.multiple_of(odd * 64, 64), 64), :].reshape(256, 2 * FH)
        for q in range(2):
            sgs[rr, :, q] = nt(xs, wrows(1 - c, q)).astype(BF16).reshape(4, 64, QW)
        send(sgs.at[rr], sgr.at[rr], g_s.at[k], g_r.at[k], sib)

    def g_line(off, k):
        pp = wrap(p + off, 4)
        arrived(sgr.at[pp], g_s.at[k], g_r.at[k])
        xs = dgu[pp].reshape(256, 2 * FH)
        return [nt(xs, wrows(c, q)).reshape(4, 64, QW) + sgr[pp, :, q].astype(F32) for q in range(2)]

    def g1():
        val = g_line(2, 0)
        for q in range(2):
            p1s[q] = val[q].astype(BF16)
            send(p1s.at[q], p1r.at[q], g_s.at[4 + q], g_r.at[4 + q], at(1 - 2 * q, 0))

    def g_2(q):
        val = g_line(1 - 2 * q, 1 + q)
        arrived(p1r.at[q], g_s.at[4 + q], g_r.at[4 + q])
        p2s[q, :, q] = (val[q] + p1r[q].astype(F32)).astype(BF16)
        p2s[q, :, 1 - q] = val[1 - q].astype(BF16)
        send(p2s.at[q], p2r.at[q], g_s.at[6 + q], g_r.at[6 + q], at(1 - 2 * q, 0))

    def g3():
        val = g_line(0, 3)
        for q in range(2):
            arrived(p2r.at[q], g_s.at[6 + q], g_r.at[6 + q])
        for q in range(2):
            g2[:, q] = val[q] + p2r[0, :, q].astype(F32) + p2r[1, :, q].astype(F32)
        opp = wrap(r + 2, 4)
        for q in range(2):
            q1s[q] = g2[opp, q].astype(BF16)
            send(q1s.at[q], q1r.at[q], g_s.at[8 + q], g_r.at[8 + q], at(0, 1 - 2 * q))

    def g4():
        for q in range(2):
            rr = wrap(r + 1 - 2 * q, 4)
            arrived(q1r.at[q], g_s.at[8 + q], g_r.at[8 + q])
            q2s[q, q] = (g2[rr, q] + q1r[q].astype(F32)).astype(BF16)
            q2s[q, 1 - q] = g2[rr, 1 - q].astype(BF16)
            send(q2s.at[q], q2r.at[q], g_s.at[10 + q], g_r.at[10 + q], at(0, 1 - 2 * q))

    def g5():
        for q in range(2):
            arrived(q2r.at[q], g_s.at[10 + q], g_r.at[10 + q])
        fin[...] = (g2[r] + q2r[0].astype(F32) + q2r[1].astype(F32)).astype(BF16)
        send(fin.at[:, other, :], fing.at[c], g_s.at[12], g_r.at[12], sib)

    def g6():
        fing[c] = fin[:, mine, :]
        arrived(fing.at[1 - c], g_s.at[12], g_r.at[12])
        for h in range(2):
            for q in range(2):
                gt_ref[:, (h * 2 + q) * QW:(h * 2 + q + 1) * QW] = nn(place, fing[h, q]).astype(BF16)
        write(gt_ref, gt_hbm, 3)

    def r_send(k):
        send(rps.at[k], rpr.at[k], rt_s.at[k], rt_r.at[k], hyper[k])

    def r_got(k):
        arrived(rpr.at[k], rt_s.at[k], rt_r.at[k])
        rps[k + 1] = rps[k] + rpr[k]

    def r_out():
        total = rps[5, pl.ds(y * 4 + x, 1), :]
        column = jnp.broadcast_to(total, (n, n)).T
        lanes = (slot_r + (c * SL).astype(F32) == row_i.astype(F32)) & (routed_r > 0.5)
        summed = jnp.sum(jnp.where(lanes, column, 0.0), axis=0, keepdims=True)
        gr_ref[...] = jnp.where(routed > 0.5, summed / jnp.maximum(prob, 0.25), 0.0)
        write(gr_ref, gr_hbm, 4)

    swapped(0, tok_rows, 0)
    T[BEGIN]()
    pack_cot()
    swapped(1, cot_rows, 0)
    C1[BEGIN]()
    T[FIRST]()
    T[SECOND]()
    T[NEAR](0)
    T[NEAR](1)
    T[NEAR](2)
    T[NEAR](3)
    T[FAR](1)
    C1[FIRST]()
    T[FAR](0)
    T[FAR](2)
    C1[NEAR](0)
    T[FAR](3)
    swapped(0, tok_rows, 1)
    T[FROM_SIB]()
    for cp in wcopies:
        cp.wait()
    fwd(0)
    C1[SECOND]()
    fwd(1)
    C2[BEGIN]()
    C1[NEAR](1)
    fwd(2)
    activate(0)
    C1[NEAR](3)
    C1[NEAR](2)
    fwd(3)
    activate(1)
    activate(2)
    C1[FAR](0)
    activate(3)
    C1[FAR](1)
    C1[FAR](2)
    C1[FAR](3)
    swapped(1, cot_rows, 1)
    C1[FROM_SIB]()
    z_down(1)
    C2[FIRST]()
    C2[NEAR](0)
    back_part(0, 1)
    C2[SECOND]()
    z_down(2)
    back_part(0, 0)
    C2[NEAR](1)
    back_part(0, 2)
    C2[NEAR](2)
    C2[NEAR](3)
    back_part(0, 3)
    C2[FAR](0)
    C2[FAR](1)
    C2[FAR](2)
    C2[FAR](3)
    C2[FROM_SIB]()
    z_down(3)
    for i in range(4):
        back_part(1, i)
        gradients(2 * i)
        gradients(2 * i + 1)
    z_pre(1)
    z_step(1)
    r_send(0)
    g_sib(0)
    g1()
    z_down(4)
    z_pre(2)
    r_got(0)
    r_send(1)
    g_sib(1)
    z_step(2)
    g_sib(2)
    g_sib(3)
    z_pre(3)
    r_got(1)
    r_send(2)
    g_2(0)
    g_2(1)
    z_step(3)
    z_pre(4)
    r_got(2)
    r_send(3)
    z_last(4)
    z_last(5)
    g3()
    z_step(4)
    z_pre(5)
    r_got(3)
    r_send(4)
    g4()
    z_out(2)
    r_got(4)
    r_out()
    g5()
    g6()
    for k in range(4):
        z_last(k)
    z_out(0)
    z_out(1)
    for cp in written:
        cp.wait()
    for cp in sent:
        cp.wait_send()


def copies(*refs):
    ins, outs, held, sem = refs[:5], refs[5:10], refs[10:15], refs[15]
    reads = [pltpu.make_async_copy(a, h, sem.at[0, k]) for k, (a, h) in enumerate(zip(ins, held))]
    writes = [pltpu.make_async_copy(h, b, sem.at[1, k]) for k, (h, b) in enumerate(zip(held, outs))]
    for cp in reads:
        cp.start()
    for read, write in zip(reads, writes):
        read.wait()
        write.start()
    for cp in writes:
        cp.wait()


def hand_over(*arrays):
    hbm = pl.BlockSpec(memory_space=pl.ANY)
    return pl.pallas_call(
        copies,
        out_shape=tuple(jax.ShapeDtypeStruct(a.shape, a.dtype) for a in arrays),
        in_specs=[hbm] * 5,
        out_specs=(hbm,) * 5,
        scratch_shapes=[pltpu.VMEM(a.shape, a.dtype) for a in arrays] + [pltpu.SemaphoreType.DMA((2, 5))],
        compiler_params=pltpu.CompilerParams(vmem_limit_bytes=62 * 1024 * 1024),
    )(*arrays)


def shards(
    tokens, cotangent, route_ids, route_weight, segment_ids, gate_weight, up_weight, down_weight
):
    vmem = pl.BlockSpec(memory_space=pltpu.VMEM)
    hbm = pl.BlockSpec(memory_space=pl.ANY)
    d = tokens.shape[2]
    dma = pltpu.SemaphoreType.DMA
    scratch = [
        pltpu.VMEM((128, d), BF16),
        pltpu.VMEM((128, d), BF16),
        pltpu.VMEM((128, d), BF16),
        pltpu.VMEM((1, 128), F32),
        pltpu.VMEM((3, 192, 2 * FH), F32),
        pltpu.VMEM((2, 16, 2, 64, QW), BF16),
        pltpu.VMEM((2, 2, 16, 2, 64, ZW), BF16),
        pltpu.VMEM((16, 8, 128), F32),
        pltpu.VMEM((d, 2 * FH), BF16),
        pltpu.VMEM((d, FH), BF16),
        pltpu.VMEM((1024, 2 * FH), F32),
        pltpu.VMEM((1024, FH), F32),
        pltpu.VMEM((1024, FH), F32),
        pltpu.VMEM((4, 2, 128, 2 * FH), BF16),
        pltpu.VMEM((3 * FH, 1024), BF16),
        pltpu.VMEM((2, NZ // 2, 3, FH, ZW), BF16),
        pltpu.VMEM((2, NZ // 2, 3, FH, ZW), BF16),
        pltpu.VMEM((4, 4, 2, 64, QW), BF16),
        pltpu.VMEM((4, 4, 2, 64, QW), BF16),
        pltpu.VMEM((2, 4, 64, QW), BF16),
        pltpu.VMEM((2, 4, 64, QW), BF16),
        pltpu.VMEM((2, 4, 2, 64, QW), BF16),
        pltpu.VMEM((2, 4, 2, 64, QW), BF16),
        pltpu.VMEM((4, 2, 64, QW), F32),
        pltpu.VMEM((2, 64, QW), BF16),
        pltpu.VMEM((2, 64, QW), BF16),
        pltpu.VMEM((2, 2, 64, QW), BF16),
        pltpu.VMEM((2, 2, 64, QW), BF16),
        pltpu.VMEM((2, 64, QW), BF16),
        pltpu.VMEM((2, 2, SL, QW), BF16),
        pltpu.VMEM((6, 16, 128), F32),
        pltpu.VMEM((5, 16, 128), F32),
        pltpu.VMEM((6, ZW, FH // 2), F32),
        pltpu.VMEM((6, 192, FH // 2), BF16),
        pltpu.VMEM((6, 192, FH // 2), BF16),
        dma((2,)),
        dma((5,)),
        dma((3,)),
        dma((3, 20)), dma((3, 20)),
        dma((3, 15)), dma((3, 15)),
        dma((2, 2)), dma((2, 2)),
        dma((15,)), dma((15,)),
        dma((2, NZ // 2, 5)), dma((2, NZ // 2, 5)),
        dma((13,)), dma((13,)),
        dma((5,)), dma((5,)),
        dma((6,)), dma((6,)),
    ]
    shape = jax.ShapeDtypeStruct
    grads = shape((192, 2 * FH), F32)
    gt, gr, gg, gu, gd = pl.pallas_call(
        kernel,
        out_shape=(shape((128, d), BF16), shape((1, 128), F32), grads, grads, grads),
        in_specs=[vmem] * 3 + [hbm] * 5,
        out_specs=(hbm,) * 5,
        scratch_shapes=scratch,
        compiler_params=pltpu.CompilerParams(
            collective_id=0, has_side_effects=True, vmem_limit_bytes=62 * 1024 * 1024),
        cost_estimate=pl.CostEstimate(
            flops=13 * 10**9, bytes_accessed=14 * 10**6, transcendentals=1024 * FH),
    )(route_ids[0].T, route_weight[0].T, segment_ids, tokens[0], cotangent[0],
      gate_weight, up_weight, down_weight)
    gt, gr, gg, gu, gd = hand_over(gt, gr, gg, gu, gd)
    return gt[None], gr, gg, gu, gd


def solution(mesh):
    return jax.shard_map(
        shards,
        mesh=mesh,
        in_specs=(
            P("dp", "et", None),
            P("dp", "et", None),
            P("dp", "et", None),
            P("dp", "et", None),
            P("dp", "et"),
            P(None, "et"),
            P(None, "et"),
            P(None, "et"),
        ),
        out_specs=(P("dp", "et", None), P("dp", "et"), P("dp", "et"), P("dp", "et"), P("dp", "et")),
        check_vma=False,
    )
```

```python
import jax
import jax.numpy as jnp
from jax import lax
from jax.experimental import pallas as pl
from jax.experimental.pallas import tpu as pltpu
from jax.sharding import PartitionSpec as P

MESH = pl.DeviceIdType.MESH
F32 = jnp.float32
BF16 = jnp.bfloat16
NZ = 8
QW = 768
ZW = 384
FH = 256
SL = 32
FAR_FIRST = ((4, 3, -3, 2), (-2, 1, -1, 0))


def nn(a, b):
    return jnp.dot(a, b, preferred_element_type=F32)


def nt(a, b):
    return lax.dot_general(a, b, (((1,), (1,)), ((), ())), preferred_element_type=F32)


def wrap(v, n):
    return lax.rem(v + 2 * n, n)


def kernel(
    ids_ref, rw_ref, seg_ref, tok_hbm, cot_hbm, wg_hbm, wu_hbm, wd_hbm,
    gt_hbm, gr_hbm, gg_hbm, gu_hbm, gd_hbm,
    tok_ref, cot_ref, picked, gt_ref, gr_ref, wob,
    tb, cb, cnts, wgu, wd, pre, hidb, backb, dgu, dT, zs, zr, sgs, sgr, p1s, p1r, p2s, p2r, g2,
    q1s, q1r, q2s, q2r, fin, fing, rps, rpr, fsum, fxs, fxr,
    i_sem, o_sem, w_sem, ag_s, ag_r, sib_s, sib_r, m_s, m_r, z_s, z_r, g_s, g_r, rt_s, rt_r, fx_s, fx_r,
):
    dp, et = lax.axis_index("dp"), lax.axis_index("et")
    z, yh = lax.div(dp, 2), lax.rem(dp, 2)
    yl, x, c = lax.div(et, 8), lax.rem(lax.div(et, 2), 4), lax.rem(et, 2)
    y = yh * 2 + yl
    p, r = y + c * (x - y), x + c * (y - x)

    def dev(xx, yy, zz, cc):
        return (zz * 2 + lax.div(yy, 2), lax.rem(yy, 2) * 8 + xx * 2 + cc)

    def at(dp_, dr_):
        pp, rr = wrap(p + dp_, 4), wrap(r + dr_, 4)
        return dev(rr + c * (pp - rr), pp + c * (rr - pp), z, c)

    def pos(dp_, dr_):
        return wrap(p + dp_, 4) * 4 + wrap(r + dr_, 4)

    sib = dev(x, y, z, 1 - c)
    zplus, zminus = dev(x, y, wrap(z + 1, NZ), c), dev(x, y, wrap(z - 1, NZ), c)

    def flip(v, bit):
        return v + bit - 2 * bit * lax.rem(lax.div(v, bit), 2)

    hyper = [sib, dev(flip(x, 1), y, z, c), dev(flip(x, 2), y, z, c),
             dev(x, flip(y, 1), z, c), dev(x, flip(y, 2), z, c)]
    partner = hyper[4]

    icopies = [pltpu.make_async_copy(tok_hbm, tok_ref, i_sem.at[0]),
               pltpu.make_async_copy(cot_hbm, cot_ref, i_sem.at[1])]
    for cp in icopies:
        cp.start()

    half = pl.ds(pl.multiple_of(yh * FH, FH), FH)
    wcopies = [
        pltpu.make_async_copy(wg_hbm.at[:, half], wgu.at[:, pl.ds(0, FH)], w_sem.at[0]),
        pltpu.make_async_copy(wu_hbm.at[:, half], wgu.at[:, pl.ds(FH, FH)], w_sem.at[1]),
        pltpu.make_async_copy(wd_hbm.at[:, half], wd, w_sem.at[2]),
    ]
    barrier = pltpu.get_barrier_semaphore()
    group = [dev(wrap(x + a, 4), yh * 2 + wrap(yl + b, 2), z, wrap(c + e, 2))
             for a in range(4) for b in range(2) for e in range(2)][1:]
    outer = dev(x, wrap(y + 2 * yl - 1, 4), z, c)
    for nb in (*group, outer, partner, zplus, zminus):
        pl.semaphore_signal(barrier, inc=1, device_id=nb, device_id_type=MESH)
    for cp in wcopies:
        cp.start()

    sent = []
    written = []

    def write(src, dst, k):
        cp = pltpu.make_async_copy(src, dst, o_sem.at[k])
        cp.start()
        written.append(cp)

    def copy(src, dst, ss, rs, to):
        return pltpu.make_async_remote_copy(
            src_ref=src, dst_ref=dst, send_sem=ss, recv_sem=rs, device_id=to, device_id_type=MESH)

    def send(src, dst, ss, rs, to):
        cp = copy(src, dst, ss, rs, to)
        cp.start()
        sent.append(cp)

    def arrived(ref, ss, rs):
        copy(ref, ref, ss, rs, sib).wait_recv()

    n = 128
    row_i = lax.broadcasted_iota(jnp.int32, (n, n), 0)
    col_i = lax.broadcasted_iota(jnp.int32, (n, n), 1)
    chosen = ids_ref[...] == 0
    routed = jnp.max(chosen.astype(F32), axis=0, keepdims=True)
    prob = jnp.sum(jnp.where(chosen, rw_ref[...].astype(F32), 0.0), axis=0, keepdims=True)
    routed_r = jnp.broadcast_to(routed, (n, n))
    routed_c = routed_r.T
    before = (row_i < col_i).astype(F32).astype(BF16)
    after = (col_i < row_i).astype(F32).astype(BF16)
    slot_r = nn(routed_r.astype(BF16), before)
    slot_c = nn(after, routed_c.astype(BF16))
    pick = jnp.where((slot_r == row_i.astype(F32)) & (routed_r > 0.5), 1.0, 0.0)[:SL].astype(BF16)
    place = jnp.where((slot_c == col_i.astype(F32)) & (routed_c > 0.5), 1.0, 0.0)[:, :SL].astype(BF16)
    seg = jnp.broadcast_to(seg_ref[...], (n, n))
    member = jnp.where(seg == row_i, 1.0, 0.0).astype(BF16)
    cnts[et] = nt(jnp.ones((8, n), BF16), member)

    mine = pl.ds(pl.multiple_of(c * SL, SL), SL)
    other = pl.ds(pl.multiple_of((1 - c) * SL, SL), SL)
    here = p * 4 + r

    icopies[0].wait()
    for q in range(4):
        tb[c, here, q] = nn(pick, tok_ref[:, q * QW:(q + 1) * QW]).astype(BF16)
    icopies[1].wait()
    for q in range(4):
        picked[:, q * QW:(q + 1) * QW] = nn(pick, cot_ref[:, q * QW:(q + 1) * QW]).astype(BF16)
    slot_member = nt(pick, member)
    slot_prob = jnp.sum(nt(pick, jnp.where(row_i == 16, prob, 0.0).astype(BF16)), axis=1, keepdims=True)

    pl.semaphore_wait(barrier, len(group) + 4)

    def send_counts():
        for k, nb in enumerate(group):
            send(cnts.at[et], cnts.at[et], m_s.at[k], m_r.at[k], nb)

    def pack_cot(i):
        if i == 0:
            for k, nb in enumerate(group):
                arrived(cnts.at[0], m_s.at[k], m_r.at[k])
        total = jnp.sum(cnts[...], axis=0)[0:1]
        slot_count = jnp.sum(slot_member * total, axis=1, keepdims=True)
        scale = jnp.where(slot_count > 0.0, slot_prob / jnp.maximum(slot_count, 1.0), 0.0)
        for j in range(4):
            cols = pl.ds(pl.multiple_of(wrap(z + FAR_FIRST[i][j], NZ) * ZW, 128), ZW)
            cb[i, c, here, j] = (picked[:, cols].astype(F32) * scale).astype(BF16)

    line = (0, -1, 1, 2)

    def ag(t, at_core):
        def ref_of(h, place_, q):
            return at_core(h, place_) if q is None else at_core(h, place_, q)

        def one(dst_p, dst_r, q, k, to):
            ref = ref_of(c, pos(dst_p, dst_r), q)
            send(ref, ref, ag_s.at[t, k], ag_r.at[t, k], to)

        def got(dst_p, dst_r, q, k):
            arrived(ref_of(c, pos(dst_p, dst_r), q), ag_s.at[t, k], ag_r.at[t, k])

        def to_sib(a, b):
            k = (a % 4) * 4 + b % 4
            send(at_core(c, pos(a, b)), at_core(c, wrap(r + b, 4) * 4 + wrap(p + a, 4)),
                 sib_s.at[t, k], sib_r.at[t, k], sib)

        def out_p(j):
            one(0, line[j], None, 4 + 4 * j, at(1, 0))
            one(0, line[j], None, 5 + 4 * j, at(-1, 0))

        def begin():
            one(0, 0, None, 0, at(0, 1))
            one(0, 0, None, 1, at(0, -1))
            out_p(0)
            to_sib(0, 0)

        def first():
            got(0, -1, None, 0)
            one(0, -1, 0, 2, at(0, 1))
            out_p(1)
            to_sib(0, -1)
            got(0, 1, None, 1)
            one(0, 1, 1, 3, at(0, -1))
            out_p(2)
            to_sib(0, 1)

        def second():
            got(0, 2, 0, 2)
            got(0, 2, 1, 3)
            out_p(3)
            to_sib(0, 2)

        def near(j):
            got(-1, line[j], None, 4 + 4 * j)
            one(-1, line[j], 0, 6 + 4 * j, at(1, 0))
            to_sib(-1, line[j])
            got(1, line[j], None, 5 + 4 * j)
            one(1, line[j], 1, 7 + 4 * j, at(-1, 0))
            to_sib(1, line[j])

        def far(j):
            got(2, line[j], 0, 6 + 4 * j)
            got(2, line[j], 1, 7 + 4 * j)
            to_sib(2, line[j])

        def from_sib():
            for a in range(4):
                for b in range(4):
                    k = a * 4 + b
                    arrived(at_core(1 - c, pos(b, a)), sib_s.at[t, k], sib_r.at[t, k])

        return begin, first, second, near, far, from_sib

    def tok_at(h, i, q=None):
        return tb.at[h, i] if q is None else tb.at[h, i, pl.ds(2 * q, 2)]

    def cot_at(k):
        return lambda h, i, q=None: cb.at[k, h, i] if q is None else cb.at[k, h, i, pl.ds(2 * q, 2)]

    T, C1, C2 = ag(0, tok_at), ag(1, cot_at(0)), ag(2, cot_at(1))
    BEGIN, FIRST, SECOND, NEAR, FAR, FROM_SIB = range(6)

    def fwd(i):
        rows = pl.ds(pl.multiple_of(i * 256, 256), 256)
        acc = None
        for q in range(4):
            xs = tb[i // 2, pl.ds(i % 2 * 8, 8), q].reshape(256, QW)
            one = nn(xs, wgu[q * QW:(q + 1) * QW, :])
            acc = one if acc is None else acc + one
        pre[rows, :] = acc

    def activate(i):
        for j in (2 * i, 2 * i + 1):
            rows = pl.ds(j * n, n)
            gate, up = pre[rows, 0:FH], pre[rows, FH:2 * FH]
            sg = 0.5 * jnp.tanh(0.5 * gate) + 0.5
            act = gate * sg
            hid = act * up
            pre[rows, 0:FH] = up * (sg * (1.0 + gate * (1.0 - sg)))
            pre[rows, FH:2 * FH] = act
            hidb[rows, :] = hid
            dT[2 * FH:3 * FH, rows] = hid.astype(BF16).T

    def back_part(k, i):
        rows = pl.ds(i * 256, 256)
        acc = None
        for j in range(4):
            xs = cb[k, i // 2, pl.ds(i % 2 * 8, 8), j].reshape(256, ZW)
            one = nn(xs, wd[pl.ds(pl.multiple_of(wrap(z + FAR_FIRST[k][j], NZ) * ZW, ZW), ZW), :])
            acc = one if acc is None else acc + one
        if k == 0:
            backb[rows, :] = acc
        else:
            backb[rows, :] += acc

    lane1 = lax.broadcasted_iota(jnp.int32, (1, n), 1)

    def gradients(j):
        rows = pl.ds(j * n, n)
        back = backb[rows, :]
        dg, du = back * pre[rows, 0:FH], back * pre[rows, FH:2 * FH]
        dg, du = dg.astype(BF16), du.astype(BF16)
        dgu[j // 4, j % 4, :, :, 0:FH] = dg.reshape(4, SL, FH)
        dgu[j // 4, j % 4, :, :, FH:2 * FH] = du.reshape(4, SL, FH)
        dT[0:FH, rows] = dg.T
        dT[FH:2 * FH, rows] = du.T

    def route_part(j):
        rows = pl.ds(j * n, n)
        rp = jnp.sum(hidb[rows, :] * backb[rows, :], axis=1, keepdims=True)
        rp_row = jnp.broadcast_to(rp, (n, n)).T[0:1]
        k, pp = j // 4, j % 4
        for rr in range(4):
            chip = pp * 4 + rr + c * (rr * 4 + pp - pp * 4 - rr)
            shift = (k * SL - rr * SL) % n
            row = rp_row if shift == 0 else pltpu.roll(rp_row, shift, 1)
            row = jnp.where((lane1 >= k * SL) & (lane1 < (k + 1) * SL), row, 0.0)
            if k == 0:
                rps[0, pl.ds(chip, 1), :] = row
            else:
                rps[0, pl.ds(chip, 1), :] += row

    def part(u, d):
        k = 0 if d in FAR_FIRST[0] else 1
        xs = cb[k, :, :, FAR_FIRST[k].index(d)].reshape(1024, ZW)
        return nn(dT[u * FH:(u + 1) * FH, :], xs)

    HF = FH // 2
    STEPS = NZ // 2
    OFFS = {k: (STEPS + 1 - k, k - STEPS - 1) for k in range(1, STEPS + 1)}
    ways = ((0, zplus), (1, zminus))
    myrows = pl.ds(pl.multiple_of(yh * 192, 192), 192)
    yourrows = pl.ds(pl.multiple_of((1 - yh) * 192, 192), 192)

    def z_down(s):
        if s == 1:
            val = part(2, STEPS).astype(BF16)
        for dr, to in ways:
            lo, hi = dr * HF, (dr + 1) * HF
            sems = (z_s.at[dr, s - 1, 4], z_r.at[dr, s - 1, 4])
            if s == 1:
                zs[dr, 0, 2, lo:hi, :] = val[lo:hi]
                ref = (dr, 0, 2, pl.ds(lo, HF))
            else:
                ref = (dr, s - 1, 2)
                own = part(2, OFFS[s][dr])
                if s == 2:
                    got = zr.at[dr, 0, 2, pl.ds(lo, HF)]
                    arrived(got, z_s.at[dr, 0, 4], z_r.at[dr, 0, 4])
                    zs[dr, 1, 2, lo:hi, :] = (own[lo:hi] + got[...].astype(F32)).astype(BF16)
                    zs[dr, 1, 2, HF - lo:FH - lo, :] = own[HF - lo:FH - lo].astype(BF16)
                else:
                    got = zr.at[dr, s - 2, 2]
                    arrived(got, z_s.at[dr, s - 2, 4], z_r.at[dr, s - 2, 4])
                    zs[dr, s - 1, 2] = (own + got[...].astype(F32)).astype(BF16)
            send(zs.at[ref], zr.at[ref], *sems, to)

    def gu_part(off):
        d = wrap(z + off, NZ)
        cols = pl.ds(pl.multiple_of(lax.rem(d, 2) * ZW, 128), ZW)
        xs = tb[:, :, lax.div(d, 2), :, cols].reshape(1024, ZW)
        return nn(dT[0:2 * FH, :], xs)

    def z_pre(s):
        offs = (STEPS,) if s == 1 else (0,) if s > STEPS else OFFS[s]
        for k, off in enumerate(offs):
            pre[k * 512:(k + 1) * 512, 0:ZW] = gu_part(off)

    def z_piece(s, k):
        u, rows = k // 2, pl.ds(k % 2 * HF, HF)
        for dr, to in ways:
            if s == 1 and k % 2 != dr:
                continue
            base = 0 if s == 1 else dr * 512
            val = pre[base + k * HF:base + (k + 1) * HF, 0:ZW]
            if s > 2 or (s == 2 and k % 2 == dr):
                got = zr.at[dr, s - 2, u, rows]
                arrived(got, z_s.at[dr, s - 2, k], z_r.at[dr, s - 2, k])
                val = val + got[...].astype(F32)
            ref = (dr, s - 1, u, rows)
            zs[ref] = val.astype(BF16)
            send(zs.at[ref], zr.at[ref], z_s.at[dr, s - 1, k], z_r.at[dr, s - 1, k], to)

    def z_step(s):
        for k in range(4):
            z_piece(s, k)

    outs = (gg_hbm, gu_hbm, gd_hbm)

    def z_last(k):
        u, lo = k // 2, k % 2 * HF
        if u == 2:
            xs = cb[1, :, :, FAR_FIRST[1].index(0)].reshape(1024, ZW)
            val = nn(dT[k * HF:(k + 1) * HF, :], xs)
        else:
            val = pre[k * HF:(k + 1) * HF, 0:ZW]
        for dr in range(2):
            got = zr.at[dr, STEPS - 1, u, pl.ds(lo, HF)]
            if u < 2:
                arrived(got, z_s.at[dr, STEPS - 1, k], z_r.at[dr, STEPS - 1, k])
            elif k == 4:
                arrived(zr.at[dr, STEPS - 1, u], z_s.at[dr, STEPS - 1, 4], z_r.at[dr, STEPS - 1, 4])
            val = val + got[...].astype(F32)
        fsum[k] = val.T
        fxs[k] = fsum[k, yourrows, :].astype(BF16)
        send(fxs.at[k], fxr.at[k], fx_s.at[k], fx_r.at[k], partner)
        wob[u, :, pl.ds(pl.multiple_of(yh * FH + lo, HF), HF)] = fsum[k, myrows, :]

    def z_out(k):
        u, lo = k // 2, k % 2 * HF
        arrived(fxr.at[k], fx_s.at[k], fx_r.at[k])
        wob[u, :, pl.ds(pl.multiple_of((1 - yh) * FH + lo, HF), HF)] = fxr[k].astype(F32)
        if k % 2:
            write(wob.at[u], outs[u], u)

    def wrows(h, q):
        return wgu[pl.ds(pl.multiple_of((h * 2 + q) * QW, QW), QW), :]

    def g_sib(k):
        rr = wrap(r + (2, 1, -1, 0)[k], 4)
        xs = dgu[:, :, rr].reshape(256, 2 * FH)
        for q in range(2):
            val = nt(xs, wrows(1 - c, q)).astype(BF16).reshape(2, 4, SL, QW)
            for k2 in range(2):
                sgs[rr, :, q, k2 * SL:(k2 + 1) * SL, :] = val[k2]
        send(sgs.at[rr], sgr.at[rr], g_s.at[k], g_r.at[k], sib)

    def g_line(off, k):
        pp = wrap(p + off, 4)
        arrived(sgr.at[pp], g_s.at[k], g_r.at[k])
        xs = dgu[:, pp].reshape(256, 2 * FH)
        out = []
        for q in range(2):
            val = nt(xs, wrows(c, q)).reshape(2, 4, SL, QW)
            out.append(jnp.concatenate([val[0], val[1]], axis=1) + sgr[pp, :, q].astype(F32))
        return out

    def g1():
        val = g_line(2, 0)
        for q in range(2):
            p1s[q] = val[q].astype(BF16)
            send(p1s.at[q], p1r.at[q], g_s.at[4 + q], g_r.at[4 + q], at(1 - 2 * q, 0))

    def g_2(q):
        val = g_line(1 - 2 * q, 1 + q)
        arrived(p1r.at[q], g_s.at[4 + q], g_r.at[4 + q])
        p2s[q, :, q] = (val[q] + p1r[q].astype(F32)).astype(BF16)
        p2s[q, :, 1 - q] = val[1 - q].astype(BF16)
        send(p2s.at[q], p2r.at[q], g_s.at[6 + q], g_r.at[6 + q], at(1 - 2 * q, 0))

    def g3():
        val = g_line(0, 3)
        for q in range(2):
            arrived(p2r.at[q], g_s.at[6 + q], g_r.at[6 + q])
        for q in range(2):
            g2[:, q] = val[q] + p2r[0, :, q].astype(F32) + p2r[1, :, q].astype(F32)
        opp = wrap(r + 2, 4)
        for q in range(2):
            q1s[q] = g2[opp, q].astype(BF16)
            send(q1s.at[q], q1r.at[q], g_s.at[8 + q], g_r.at[8 + q], at(0, 1 - 2 * q))

    def g4():
        for q in range(2):
            rr = wrap(r + 1 - 2 * q, 4)
            arrived(q1r.at[q], g_s.at[8 + q], g_r.at[8 + q])
            q2s[q, q] = (g2[rr, q] + q1r[q].astype(F32)).astype(BF16)
            q2s[q, 1 - q] = g2[rr, 1 - q].astype(BF16)
            send(q2s.at[q], q2r.at[q], g_s.at[10 + q], g_r.at[10 + q], at(0, 1 - 2 * q))

    def g5():
        for q in range(2):
            arrived(q2r.at[q], g_s.at[10 + q], g_r.at[10 + q])
        fin[...] = (g2[r] + q2r[0].astype(F32) + q2r[1].astype(F32)).astype(BF16)
        send(fin.at[:, other, :], fing.at[c], g_s.at[12], g_r.at[12], sib)

    def g6():
        fing[c] = fin[:, mine, :]
        arrived(fing.at[1 - c], g_s.at[12], g_r.at[12])
        for h in range(2):
            for q in range(2):
                gt_ref[:, (h * 2 + q) * QW:(h * 2 + q + 1) * QW] = nn(place, fing[h, q]).astype(BF16)
        write(gt_ref, gt_hbm, 3)

    def r_send(k):
        send(rps.at[k], rpr.at[k], rt_s.at[k], rt_r.at[k], hyper[k])

    def r_got(k):
        arrived(rpr.at[k], rt_s.at[k], rt_r.at[k])
        rps[k + 1] = rps[k] + rpr[k]

    def r_out():
        total = rps[5, pl.ds(y * 4 + x, 1), :]
        column = jnp.broadcast_to(total, (n, n)).T
        lanes = (slot_r + (c * SL).astype(F32) == row_i.astype(F32)) & (routed_r > 0.5)
        summed = jnp.sum(jnp.where(lanes, column, 0.0), axis=0, keepdims=True)
        gr_ref[...] = jnp.where(routed > 0.5, summed / jnp.maximum(prob, 0.25), 0.0)
        write(gr_ref, gr_hbm, 4)

    T[BEGIN]()
    send_counts()
    pack_cot(0)
    C1[BEGIN]()
    T[FIRST]()
    T[NEAR](0)
    T[SECOND]()
    T[NEAR](1)
    T[NEAR](2)
    T[NEAR](3)
    pack_cot(1)
    C2[BEGIN]()
    T[FAR](0)
    C1[FIRST]()
    C1[NEAR](0)
    T[FAR](1)
    T[FAR](2)
    C1[SECOND]()
    T[FAR](3)
    T[FROM_SIB]()
    for cp in wcopies:
        cp.wait()
    C1[NEAR](1)
    C1[NEAR](2)
    fwd(0)
    C1[NEAR](3)
    C2[FIRST]()
    C2[NEAR](0)
    fwd(1)
    C1[FAR](0)
    C1[FAR](1)
    fwd(2)
    C1[FAR](2)
    C2[SECOND]()
    fwd(3)
    C1[FAR](3)
    activate(0)
    activate(1)
    C2[NEAR](1)
    C2[NEAR](2)
    activate(2)
    activate(3)
    C1[FROM_SIB]()
    z_down(1)
    C2[NEAR](3)
    back_part(0, 0)
    back_part(0, 1)
    C2[FAR](0)
    back_part(0, 2)
    back_part(0, 3)
    z_down(2)
    C2[FAR](1)
    C2[FAR](2)
    C2[FAR](3)
    C2[FROM_SIB]()
    for i in range(4):
        back_part(1, i)
        gradients(2 * i)
        gradients(2 * i + 1)
    z_pre(1)
    z_step(1)
    g_sib(0)
    z_down(3)
    g1()
    z_pre(2)
    g_sib(1)
    z_step(2)
    for j in range(8):
        route_part(j)
    r_send(0)
    z_down(4)
    g_sib(2)
    g_sib(3)
    z_pre(3)
    r_got(0)
    r_send(1)
    g_2(0)
    g_2(1)
    r_got(1)
    r_send(2)
    z_step(3)
    z_pre(4)
    r_got(2)
    r_send(3)
    z_last(4)
    z_last(5)
    g3()
    z_step(4)
    z_pre(5)
    r_got(3)
    r_send(4)
    g4()
    z_out(4)
    z_out(5)
    r_got(4)
    r_out()
    g5()
    g6()
    for k in range(4):
        z_last(k)
    for k in range(4):
        z_out(k)
    for cp in written:
        cp.wait()
    for cp in sent:
        cp.wait_send()


def copies(*refs):
    ins, outs, held, sem = refs[:5], refs[5:10], refs[10:15], refs[15]
    reads = [pltpu.make_async_copy(a, h, sem.at[0, k]) for k, (a, h) in enumerate(zip(ins, held))]
    writes = [pltpu.make_async_copy(h, b, sem.at[1, k]) for k, (h, b) in enumerate(zip(held, outs))]
    for cp in reads:
        cp.start()
    for read, write in zip(reads, writes):
        read.wait()
        write.start()
    for cp in writes:
        cp.wait()


def hand_over(*arrays):
    hbm = pl.BlockSpec(memory_space=pl.ANY)
    return pl.pallas_call(
        copies,
        out_shape=tuple(jax.ShapeDtypeStruct(a.shape, a.dtype) for a in arrays),
        in_specs=[hbm] * 5,
        out_specs=(hbm,) * 5,
        scratch_shapes=[pltpu.VMEM(a.shape, a.dtype) for a in arrays] + [pltpu.SemaphoreType.DMA((2, 5))],
        compiler_params=pltpu.CompilerParams(vmem_limit_bytes=62 * 1024 * 1024),
    )(*arrays)


def shards(
    tokens, cotangent, route_ids, route_weight, segment_ids, gate_weight, up_weight, down_weight
):
    vmem = pl.BlockSpec(memory_space=pltpu.VMEM)
    hbm = pl.BlockSpec(memory_space=pl.ANY)
    d = tokens.shape[2]
    dma = pltpu.SemaphoreType.DMA
    scratch = [
        pltpu.VMEM((128, d), BF16),
        pltpu.VMEM((128, d), BF16),
        pltpu.VMEM((SL, d), BF16),
        pltpu.VMEM((128, d), BF16),
        pltpu.VMEM((1, 128), F32),
        pltpu.VMEM((3, 192, 2 * FH), F32),
        pltpu.VMEM((2, 16, 4, SL, QW), BF16),
        pltpu.VMEM((2, 2, 16, 4, SL, ZW), BF16),
        pltpu.VMEM((16, 8, 128), F32),
        pltpu.VMEM((d, 2 * FH), BF16),
        pltpu.VMEM((d, FH), BF16),
        pltpu.VMEM((1024, 2 * FH), F32),
        pltpu.VMEM((1024, FH), F32),
        pltpu.VMEM((1024, FH), F32),
        pltpu.VMEM((2, 4, 4, SL, 2 * FH), BF16),
        pltpu.VMEM((3 * FH, 1024), BF16),
        pltpu.VMEM((2, NZ // 2, 3, FH, ZW), BF16),
        pltpu.VMEM((2, NZ // 2, 3, FH, ZW), BF16),
        pltpu.VMEM((4, 4, 2, 64, QW), BF16),
        pltpu.VMEM((4, 4, 2, 64, QW), BF16),
        pltpu.VMEM((2, 4, 64, QW), BF16),
        pltpu.VMEM((2, 4, 64, QW), BF16),
        pltpu.VMEM((2, 4, 2, 64, QW), BF16),
        pltpu.VMEM((2, 4, 2, 64, QW), BF16),
        pltpu.VMEM((4, 2, 64, QW), F32),
        pltpu.VMEM((2, 64, QW), BF16),
        pltpu.VMEM((2, 64, QW), BF16),
        pltpu.VMEM((2, 2, 64, QW), BF16),
        pltpu.VMEM((2, 2, 64, QW), BF16),
        pltpu.VMEM((2, 64, QW), BF16),
        pltpu.VMEM((2, 2, SL, QW), BF16),
        pltpu.VMEM((6, 16, 128), F32),
        pltpu.VMEM((5, 16, 128), F32),
        pltpu.VMEM((6, ZW, FH // 2), F32),
        pltpu.VMEM((6, 192, FH // 2), BF16),
        pltpu.VMEM((6, 192, FH // 2), BF16),
        dma((2,)),
        dma((5,)),
        dma((3,)),
        dma((3, 20)), dma((3, 20)),
        dma((3, 16)), dma((3, 16)),
        dma((15,)), dma((15,)),
        dma((2, NZ // 2, 5)), dma((2, NZ // 2, 5)),
        dma((13,)), dma((13,)),
        dma((5,)), dma((5,)),
        dma((6,)), dma((6,)),
    ]
    shape = jax.ShapeDtypeStruct
    grads = shape((192, 2 * FH), F32)
    gt, gr, gg, gu, gd = pl.pallas_call(
        kernel,
        out_shape=(shape((128, d), BF16), shape((1, 128), F32), grads, grads, grads),
        in_specs=[vmem] * 3 + [hbm] * 5,
        out_specs=(hbm,) * 5,
        scratch_shapes=scratch,
        compiler_params=pltpu.CompilerParams(
            collective_id=0, has_side_effects=True, vmem_limit_bytes=62 * 1024 * 1024),
        cost_estimate=pl.CostEstimate(
            flops=13 * 10**9, bytes_accessed=14 * 10**6, transcendentals=1024 * FH),
    )(route_ids[0].T, route_weight[0].T, segment_ids, tokens[0], cotangent[0],
      gate_weight, up_weight, down_weight)
    gt, gr, gg, gu, gd = hand_over(gt, gr, gg, gu, gd)
    return gt[None], gr, gg, gu, gd


def solution(mesh):
    return jax.shard_map(
        shards,
        mesh=mesh,
        in_specs=(
            P("dp", "et", None),
            P("dp", "et", None),
            P("dp", "et", None),
            P("dp", "et", None),
            P("dp", "et"),
            P(None, "et"),
            P(None, "et"),
            P(None, "et"),
        ),
        out_specs=(P("dp", "et", None), P("dp", "et"), P("dp", "et"), P("dp", "et"), P("dp", "et")),
        check_vma=False,
    )
```
